32 devices in a mesh: row: 4 (over y, core), col: 8 (over z, x).
Axes of the slice: x: 2, y: 2, z: 4, core: 2. Of those that a mesh axis runs over, the one named last changes fastest.
Arguments:
- row_coords: bfloat16 [3, 4096, 512], P(None, ('row', 'col')), may hold values from -10 to 10, as said below
- col_coords: bfloat16 [3, 8192, 512], P(None, 'col'), may hold values from -10 to 10, as said below
- start_block: float32 [8192, 64], P('col'), may hold values from -0.0625 to 0.0625
Outputs:
- basis: float32 [4096, 64], P('row')
- image: float32 [8192, 64], P('col')
The draws below stay inside these ranges and needn't reach their ends.
Inputs may be any that keep to these rules, and one draw needn't show every extreme that they name: `row_coords`: coordinates of frames of one molecule in varying conformations. `col_coords`: coordinates of frames of the same molecule in varying conformations.
All inputs are finite; a program needn't handle non-finite values.
Results may differ from the reference program's by a relative error of at most 0.0073.
Values may be sent and summed in bfloat16 or wider, within the bound.
A program may use at most 128 MiB of HBM per device.

```python
import math
import jax
import jax.numpy as jnp
from jax import lax

ATOMS = 512
K = 64
NEWTON = 8
C_DEV = 1024
RF = 4096
CF = 8192
N_COL = 8


def shared_structure(key):
    base = jnp.clip(jax.random.normal(jax.random.fold_in(key, 7), (3, ATOMS), jnp.float32), -4.0, 4.0)
    base = base - jnp.mean(base, axis=1, keepdims=True)
    mode = jnp.clip(jax.random.normal(jax.random.fold_in(key, 9), (3, ATOMS), jnp.float32), -4.0, 4.0)
    mode = mode - jnp.mean(mode, axis=1, keepdims=True)
    base = base * jnp.array([2.0, 0.35, 0.25], jnp.float32)[:, None]
    mode = mode * 0.5
    return (base, mode)


def moving_frames(key, count, salt):
    base, mode = shared_structure(key)
    inner = jax.random.fold_in(key, salt)
    quats = jax.random.normal(jax.random.fold_in(inner, 1), (count, 4), jnp.float32)
    quats = quats / (jnp.sqrt(jnp.sum(quats * quats, axis=1, keepdims=True)) + 1e-06)
    qw, qx, qy, qz = (quats[:, 0], quats[:, 1], quats[:, 2], quats[:, 3])
    rotation = jnp.stack([jnp.stack([1 - 2 * (qy * qy + qz * qz), 2 * (qx * qy - qz * qw), 2 * (qx * qz + qy * qw)], axis=1), jnp.stack([2 * (qx * qy + qz * qw), 1 - 2 * (qx * qx + qz * qz), 2 * (qy * qz - qx * qw)], axis=1), jnp.stack([2 * (qx * qz - qy * qw), 2 * (qy * qz + qx * qw), 1 - 2 * (qx * qx + qy * qy)], axis=1)], axis=1)
    noise = jnp.clip(jax.random.normal(jax.random.fold_in(inner, 2), (3, count, ATOMS), jnp.float32), -4.0, 4.0)
    amplitude = jax.random.uniform(jax.random.fold_in(inner, 4), (count,), jnp.float32, -1.0, 1.0)
    shape = base[None, :, :] + amplitude[:, None, None] * mode[None, :, :]
    position = jnp.arange(count, dtype=jnp.float32) / count
    spread = jax.random.uniform(jax.random.fold_in(inner, 3), (count,), jnp.float32, 1.0, 1.6)
    jitter = jnp.exp(jax.random.uniform(jax.random.fold_in(inner, 5), (count,), jnp.float32, 0.0, 0.9162907))
    sigma = 0.2 * jnp.exp(position * 1.0986123) * spread * jitter
    rotated = jnp.einsum('fcd,fda->cfa', rotation, shape)
    moved = rotated + sigma[None, :, None] * noise
    return jnp.clip(moved, -10.0, 10.0).astype(jnp.bfloat16)


def draw_row_coords(key, part):
    return moving_frames(key, RF, 11)


def draw_col_coords(key, part):
    return moving_frames(key, CF, 13)


def block_scale(key, extent, cuts, least, largest):
    level, own = 1.0, jax.random.fold_in(key, 6)
    for dim, parts in cuts:
        steps = jnp.exp(jax.random.uniform(jax.random.fold_in(own, dim), (parts,), jnp.float32, least / len(cuts), largest / len(cuts)))
        level = level * jnp.repeat(steps, extent[dim] // parts).reshape([-1 if axis == dim else 1 for axis in range(len(extent))])
    return level


def bell_draw(rng, shape, width, limit, pieces=(), kind=jnp.bfloat16):
    loudness = block_scale(rng, shape, pieces, -0.22, 0.18) if pieces else 1.0
    values = jax.random.normal(rng, shape, jnp.float32) * width * loudness
    return jnp.minimum(jnp.maximum(values, -limit), limit).astype(kind)


def setup_inputs(seed: int = 0) -> dict:
    arg_keys = jax.random.split(jax.random.key(seed), 4)
    row_coords = draw_row_coords(jax.random.fold_in(arg_keys[3], 71), 0)
    col_coords = draw_col_coords(jax.random.fold_in(arg_keys[3], 71), 0)
    start_block = bell_draw(arg_keys[2], (CF, K), CF ** -0.5, 0.0625, ((0, 8),), jnp.float32)
    return dict(row_coords=row_coords, col_coords=col_coords, start_block=start_block)


def centre_frames(coords):
    shifted = coords.astype(jnp.float32)
    shifted = shifted - lax.optimization_barrier(jnp.mean(shifted, axis=2, keepdims=True))
    rounded = shifted.astype(jnp.bfloat16)
    widened = lax.optimization_barrier(rounded).astype(jnp.float32)
    return (rounded, lax.optimization_barrier(jnp.sum(widened * widened, axis=(0, 2))) / ATOMS)

def two_minor(matrix, upper, lower, left, right):
    return matrix[upper][left] * matrix[lower][right] - matrix[lower][left] * matrix[upper][right]

def squared_rmsd(cross, row_norm, col_norm):
    part = [[cross[first, second] for second in range(3)] for first in range(3)]
    trace = part[0][0] + part[1][1] + part[2][2]
    matrix = [[None] * 4 for index in range(4)]
    matrix[0][0] = trace
    matrix[1][1] = 2.0 * part[0][0] - trace
    matrix[2][2] = 2.0 * part[1][1] - trace
    matrix[3][3] = 2.0 * part[2][2] - trace
    matrix[0][1] = part[1][2] - part[2][1]
    matrix[0][2] = part[2][0] - part[0][2]
    matrix[0][3] = part[0][1] - part[1][0]
    matrix[1][2] = part[0][1] + part[1][0]
    matrix[1][3] = part[2][0] + part[0][2]
    matrix[2][3] = part[1][2] + part[2][1]
    for first in range(4):
        for second in range(first):
            matrix[first][second] = matrix[second][first]
    key_determinant = two_minor(matrix, 0, 1, 0, 1) * two_minor(matrix, 2, 3, 2, 3) - two_minor(matrix, 0, 1, 0, 2) * two_minor(matrix, 2, 3, 1, 3) + two_minor(matrix, 0, 1, 0, 3) * two_minor(matrix, 2, 3, 1, 2) + two_minor(matrix, 0, 1, 1, 2) * two_minor(matrix, 2, 3, 0, 3) - two_minor(matrix, 0, 1, 1, 3) * two_minor(matrix, 2, 3, 0, 2) + two_minor(matrix, 0, 1, 2, 3) * two_minor(matrix, 2, 3, 0, 1)
    cross_determinant = part[0][0] * (part[1][1] * part[2][2] - part[1][2] * part[2][1]) - part[0][1] * (part[1][0] * part[2][2] - part[1][2] * part[2][0]) + part[0][2] * (part[1][0] * part[2][1] - part[1][1] * part[2][0])
    squares = sum((part[first][second] * part[first][second] for first in range(3) for second in range(3)))
    coeff_two = -2.0 * squares
    coeff_one = -8.0 * cross_determinant
    coeff_zero = key_determinant
    root_guess = 0.5 * (row_norm + col_norm)
    for sweep in range(NEWTON):
        poly_value = ((root_guess * root_guess + coeff_two) * root_guess + coeff_one) * root_guess + coeff_zero
        poly_slope = (4.0 * root_guess * root_guess + 2.0 * coeff_two) * root_guess + coeff_one
        root_guess = root_guess - poly_value / poly_slope
    return row_norm + col_norm - 2.0 * root_guess

def reference(row_coords, col_coords, start_block):
    highest = lax.Precision.HIGHEST
    rows, row_norm = centre_frames(row_coords)
    cols, col_norm = centre_frames(col_coords)
    rows_wide = rows.astype(jnp.float32)
    col_blocks = cols.reshape(3, N_COL, C_DEV, ATOMS).transpose(1, 0, 2, 3)
    norm_blocks = col_norm.reshape(N_COL, C_DEV)

    def tile(inputs):
        block, norms = inputs
        cross = jnp.einsum('ark,bck->abrc', rows_wide, block.astype(jnp.float32)) / ATOMS
        return squared_rmsd(cross, row_norm[:, None], norms[None, :])
    stacked = lax.map(tile, (col_blocks, norm_blocks))
    dist = stacked.transpose(1, 0, 2).reshape(RF, CF)
    row_mean = lax.optimization_barrier(jnp.sum(dist, axis=1)) / CF
    col_mean = lax.optimization_barrier(jnp.sum(dist, axis=0)) / RF
    grand = jnp.sum(row_mean) / RF
    centred = -0.5 * (dist - row_mean[:, None] - col_mean[None, :] + grand)
    panel = jnp.dot(centred, start_block, precision=highest)
    gram = jnp.dot(panel.T, panel, precision=highest) / RF
    lower = jnp.linalg.cholesky(gram)
    basis = lax.linalg.triangular_solve(lower, panel, left_side=False, lower=True, transpose_a=True)
    image = jnp.dot(centred.T, basis, precision=highest) / math.sqrt(RF)
    return (basis, image)
```

```python
import functools
import math

import jax
import jax.numpy as jnp
from jax import lax
from jax.experimental import pallas as pl
from jax.experimental.pallas import tpu as pltpu
from jax.sharding import PartitionSpec as P

NEWTON = 8
TILE = 256
MESH = pl.DeviceIdType.MESH
HIGHEST = lax.Precision.HIGHEST
F32, BF16 = jnp.float32, jnp.bfloat16


def dot_nt(left, right, precision=None):
    return lax.dot_general(
        left, right, (((1,), (1,)), ((), ())), precision=precision, preferred_element_type=F32
    )


def dot_nn(left, right, precision=None):
    return lax.dot_general(
        left, right, (((1,), (0,)), ((), ())), precision=precision, preferred_element_type=F32
    )


def split(value):
    high = value.astype(BF16)
    return high, (value - high.astype(F32)).astype(BF16)


def setup_terms(s):
    c00 = s[1][1] * s[2][2] - s[1][2] * s[2][1]
    c01 = s[1][2] * s[2][0] - s[1][0] * s[2][2]
    c02 = s[1][0] * s[2][1] - s[1][1] * s[2][0]
    c10 = s[2][1] * s[0][2] - s[2][2] * s[0][1]
    c11 = s[2][2] * s[0][0] - s[2][0] * s[0][2]
    c12 = s[2][0] * s[0][1] - s[2][1] * s[0][0]
    c20 = s[0][1] * s[1][2] - s[0][2] * s[1][1]
    c21 = s[0][2] * s[1][0] - s[0][0] * s[1][2]
    c22 = s[0][0] * s[1][1] - s[0][1] * s[1][0]
    det = s[0][0] * c00 + s[0][1] * c01 + s[0][2] * c02
    square = lambda items: functools.reduce(lambda a, b: a + b, [v * v for v in items])
    total = square([s[a][b] for a in range(3) for b in range(3)])
    cof = square([c00, c01, c02, c10, c11, c12, c20, c21, c22])
    return total, cof, -2.0 * det


def distances(items):
    coeffs = [setup_terms(s) for s, _, _ in items]
    sums = [rn + cn for _, rn, cn in items]
    lam = [0.5 * v for v in sums]
    for _ in range(NEWTON):
        for k, (total, cof, g) in enumerate(coeffs):
            x = lam[k]
            m = x * x - total
            value = 0.25 * (m * m) + (g * x - cof)
            lam[k] = x - value * pl.reciprocal(m * x + g, approx=True)
    return [v - 2.0 * x for v, x in zip(sums, lam)]


def kernel(n, nr, total_rows, total_cols, row_ref, col_ref, st_ref, basis_ref, image_ref,
           rbuf, cc, cn_ref, rn_ref, rc, s_a, s_b, d_hi, d_lo, lhs, ssb, pout, part, agb, q_ref, lhs2,
           gx, uout, ub, ib,
           ag_send, ag_recv, ss_send, ss_recv, pa_send, pa_recv, pg_send, pg_recv,
           gx_send, gx_recv, u_send, u_recv, i_send, i_recv):
    c, r = lax.axis_index("col"), lax.axis_index("row")
    line = n // 2
    z, x = c // 2, c % 2
    _, block_rows, atoms = row_ref.shape
    cols = col_ref.shape[1]
    vecs = st_ref.shape[0]
    chunk = cols // nr
    tiles = cols // TILE

    def col_dev(k):
        return (r, k)

    def row_dev(k):
        return (k, c)

    def remote(src, dst, send, recv, dev):
        return pltpu.make_async_remote_copy(
            src_ref=src, dst_ref=dst, send_sem=send, recv_sem=recv, device_id=dev, device_id_type=MESH
        )

    barrier = pltpu.get_barrier_semaphore()
    for d in range(1, n):
        pl.semaphore_signal(barrier, inc=1, device_id=col_dev((c + d) % n), device_id_type=MESH)
    for d in range(1, nr):
        pl.semaphore_signal(barrier, inc=1, device_id=row_dev((r + d) % nr), device_id_type=MESH)
    rbuf[c] = row_ref[...]
    pl.semaphore_wait(barrier, n - 1 + nr - 1)

    def hop(block, way):
        dev = col_dev((c + 1 - 2 * x, c + 2, c - 2)[way])
        return remote(rbuf.at[block], rbuf.at[block], ag_send.at[way, block], ag_recv.at[block], dev)

    def hops(block_z, act):
        block = block_z * 2 + x
        act(hop(block, 0))

        @pl.when((block_z <= z) & (z < line - 1))
        def _():
            act(hop(block, 1))

        @pl.when((block_z >= z) & (z > 0))
        def _():
            act(hop(block, 2))

    hops(z, lambda copy: copy.start())

    st = st_ref[...]
    st_hi, st_lo = split(st)
    lhs[0:vecs, :] = st_hi
    lhs[vecs:2 * vecs, :] = st_lo
    lhs[2 * vecs:2 * vecs + 16, :] = jnp.ones((16, cols), BF16)
    ssb[c] = dot_nt(jnp.ones((8, cols), F32), st, HIGHEST)

    def ss_copy(d):
        k = (c + d) % n
        return remote(ssb.at[c], ssb.at[c], ss_send.at[d], ss_recv.at[c], col_dev(k))

    for d in range(1, n):
        ss_copy(d).start()

    step_rows = 128

    def centre_cols(k, carry):
        at = pl.ds(pl.multiple_of(k * step_rows, step_rows), step_rows)
        squares = jnp.zeros((step_rows, atoms), F32)
        for b in range(3):
            v = col_ref[b, at, :].astype(F32)
            v = (v - jnp.sum(v, axis=1, keepdims=True) * (1.0 / atoms)).astype(BF16)
            cc[b, at, :] = v
            v = v.astype(F32)
            squares = squares + v * v
        cn_ref[:, at] = dot_nt(jnp.ones((8, atoms), F32), squares, HIGHEST) * (1.0 / atoms)
        return carry

    lax.fori_loop(0, cols // step_rows, centre_cols, 0)

    near = jnp.minimum(z, line - 1 - z)
    sign = jnp.where(z < line - 1 - z, 1, -1)

    def line_place(q):
        both = jnp.where(q % 2 == 1, (q + 1) // 2, -(q // 2))
        return z + jnp.where(q <= 2 * near, both, sign * (q - near))

    def part_copy(block):
        return remote(pout.at[block], part.at[c], pa_send.at[block], pa_recv.at[c], col_dev(block))

    def run_block(p, carry):
        block_z = line_place(p // 2)
        other = p % 2
        block = block_z * 2 + jnp.where(other == 1, 1 - x, x)

        @pl.when(p > 0)
        def _():
            hop(block, 0).wait_recv()

        @pl.when((p > 0) & (other == 0))
        def _():
            hops(block_z, lambda copy: copy.start())

        norm = jnp.zeros((block_rows, 1), F32)
        for a in range(3):
            v = rbuf[block, a].astype(F32)
            v = (v - jnp.sum(v, axis=1, keepdims=True) * (1.0 / atoms)).astype(BF16).astype(F32)
            norm = norm + jnp.sum(v * v, axis=1, keepdims=True)
            rc[a * block_rows:(a + 1) * block_rows, :] = (v * (1.0 / atoms)).astype(BF16)
        rn_ref[...] = jnp.broadcast_to(norm * (1.0 / atoms), (block_rows, 128))

        def cross(t, out):
            at = pl.ds(pl.multiple_of(t * TILE, TILE), TILE)
            for b in range(3):
                out[b] = dot_nt(rc[...], cc[b, at, :])

        def solve(t, src):
            for i0 in range(0, block_rows, 32):
                items, places = [], []
                for i in range(i0, i0 + 32, 8):
                    rn = rn_ref[i:i + 8, :]
                    for l in range(0, TILE, 128):
                        s = [[src[b, a * block_rows + i:a * block_rows + i + 8, l:l + 128] for b in range(3)]
                             for a in range(3)]
                        cn = cn_ref[:, pl.ds(pl.multiple_of(t * TILE + l, 128), 128)]
                        items.append((s, rn, cn))
                        places.append((i, l))
                dist = dict(zip(places, distances(items)))
                for i in range(i0, i0 + 32, 16):
                    at_rows = pl.ds(pl.multiple_of(block * block_rows + i, 16), 16)
                    for l in range(0, TILE, 128):
                        value = jnp.concatenate([dist[(i, l)], dist[(i + 8, l)]], axis=0)
                        high, low = split(value)
                        at_cols = pl.ds(pl.multiple_of(t * TILE + l, 128), 128)
                        d_hi[at_rows, at_cols] = high
                        d_lo[at_rows, at_cols] = low

        cross(0, s_a)

        def pair(k, inner):
            t = 2 * k
            cross(t + 1, s_b)
            solve(t, s_a)
            cross((t + 2) % tiles, s_a)
            solve(t + 1, s_b)
            return inner

        lax.fori_loop(0, tiles // 2, pair, 0)

        at = pl.ds(pl.multiple_of(block * block_rows, block_rows), block_rows)
        high = dot_nt(lhs[...], d_hi[at, :])
        low = dot_nt(lhs[0:vecs, :], d_lo[at, :])
        low_sum = dot_nt(lhs[2 * vecs:2 * vecs + 16, :], d_lo[at, :])
        pout[block, 0:vecs] = high[0:vecs] + high[vecs:2 * vecs] + low
        pout[block, vecs:vecs + 8] = high[2 * vecs:2 * vecs + 8] + low_sum[0:8]

        @pl.when(block == c)
        def _():
            part[c] = pout[block]

        @pl.when(block != c)
        def _():
            part_copy(block).start()

        return carry

    lax.fori_loop(0, n, run_block, 0)

    for d in range(1, n):
        k = (c + d) % n
        remote(ssb.at[k], ssb.at[k], ss_send.at[d], ss_recv.at[k], col_dev(k)).wait_recv()
        remote(pout.at[k], part.at[k], pa_send.at[k], pa_recv.at[k], col_dev(k)).wait_recv()
    summed, starts = part[0], ssb[0]
    for k in range(1, n):
        summed, starts = summed + part[k], starts + ssb[k]
    eye = lax.broadcasted_iota(jnp.int32, (vecs, vecs), 0) == lax.broadcasted_iota(jnp.int32, (vecs, vecs), 1)
    mean = jnp.sum(jnp.where(eye, jnp.broadcast_to(starts[0:1, :], (vecs, vecs)), 0.0), axis=1, keepdims=True)
    mean = mean * (1.0 / total_cols)
    agb[c, 0:vecs] = summed[0:vecs] - mean * summed[vecs:vecs + 1]
    agb[c, vecs:vecs + 8] = summed[vecs:vecs + 8]

    def pg_copy(d):
        return remote(agb.at[c], agb.at[c], pg_send.at[d], pg_recv.at[c], col_dev((c + d) % n))

    for d in range(1, n):
        pg_copy(d).start()
    for d in range(1, n):
        k = (c + d) % n
        remote(agb.at[k], agb.at[k], pg_send.at[d], pg_recv.at[k], col_dev(k)).wait_recv()

    local = n * block_rows
    for k in range(n):
        q_ref[:, k * block_rows:(k + 1) * block_rows] = agb[k]
    prod = q_ref[0:vecs, :]
    row_total = q_ref[vecs:vecs + 1, :]
    local_mean = jnp.sum(prod, axis=1, keepdims=True) * (1.0 / local)
    q = prod - local_mean
    q_ref[0:vecs, :] = q
    q_hi, q_lo = split(q)
    lhs2[0:vecs, :] = q_hi
    lhs2[vecs:2 * vecs, :] = q_lo
    lhs2[2 * vecs:2 * vecs + 16, :] = jnp.ones((16, local), BF16)
    gx[r, :, 0:vecs] = dot_nt(q, q, HIGHEST)
    lane = lax.broadcasted_iota(jnp.int32, (vecs, 128), 1)
    extra = jnp.where(lane == 0, local_mean, 0.0)
    extra = extra + jnp.where(lane == 1, jnp.sum(q * row_total, axis=1, keepdims=True), 0.0)
    extra = extra + jnp.where(lane == 2, jnp.sum(row_total, axis=1, keepdims=True), 0.0)
    gx[r, :, 128:256] = extra

    def gx_copy(d):
        return remote(gx.at[r], gx.at[r], gx_send.at[d], gx_recv.at[r], row_dev((r + d) % nr))

    for d in range(1, nr):
        gx_copy(d).start()

    def u_copy(d):
        o = (r + d) % nr
        return remote(uout.at[d], ub.at[r], u_send.at[d], u_recv.at[r], row_dev(o))

    for d in list(range(1, nr)) + [0]:
        o = (r + d) % nr
        at = pl.ds(pl.multiple_of(o * chunk, chunk), chunk)
        high = dot_nn(lhs2[...], d_hi[:, at])
        low = dot_nn(lhs2[0:vecs, :], d_lo[:, at])
        low_sum = dot_nn(lhs2[2 * vecs:2 * vecs + 16, :], d_lo[:, at])
        product = high[0:vecs] + high[vecs:2 * vecs] + low
        sums = high[2 * vecs:2 * vecs + 8] + low_sum[0:8]
        if d:
            uout[d, 0:vecs] = product
            uout[d, vecs:vecs + 8] = sums
            u_copy(d).start()
        else:
            ub[r, 0:vecs] = product
            ub[r, vecs:vecs + 8] = sums

    for d in range(1, nr):
        k = (r + d) % nr
        remote(gx.at[k], gx.at[k], gx_send.at[d], gx_recv.at[k], row_dev(k)).wait_recv()
    means = [gx[k, :, 128:129] for k in range(nr)]
    mean = sum(means) * (1.0 / nr)
    shift = jnp.zeros((vecs, 128), F32)
    gram = jnp.zeros((vecs, vecs), F32)
    weighted = jnp.zeros((vecs, 1), F32)
    for k in range(nr):
        gram = gram + gx[k, :, 0:vecs]
        shift = shift + jnp.where(lane == k, means[k] - mean, 0.0)
        weighted = weighted + gx[k, :, 129:130] + (means[k] - mean) * gx[k, :, 130:131]
    gram = (gram + float(local) * dot_nt(shift, shift, HIGHEST)) * (1.0 / total_rows)

    work = jnp.concatenate([gram, jnp.where(eye, 1.0, 0.0)], axis=1)
    below = lax.broadcasted_iota(jnp.int32, (vecs, 1), 0)
    pivots = jnp.zeros((vecs, 1), F32)
    for k in range(vecs):
        top = work[k:k + 1, :]
        pivot = top[:, k:k + 1]
        pivots = jnp.where(below == k, pivot, pivots)
        factor = jnp.where(below > k, work[:, k:k + 1], 0.0)
        work = work - factor * (top * (1.0 / pivot))
    inverse = work[:, vecs:2 * vecs] * lax.rsqrt(pivots)

    own_mean = jnp.sum(jnp.where(lane == r, shift, 0.0), axis=1, keepdims=True)
    basis_ref[...] = -dot_nn(inverse, q_ref[0:vecs, :] + own_mean, HIGHEST)

    for d in range(1, nr):
        k = (r + d) % nr
        remote(uout.at[d], ub.at[k], u_send.at[d], u_recv.at[k], row_dev(k)).wait_recv()
    gathered = jnp.broadcast_to(weighted * (-1.0 / total_cols), (vecs, chunk))
    for k in range(nr):
        gathered = gathered + (ub[k, 0:vecs] + (means[k] - mean) * ub[k, vecs:vecs + 1])
    ib[r] = dot_nn(inverse, gathered, HIGHEST) * (0.5 / math.sqrt(total_rows))

    def i_copy(d):
        return remote(ib.at[r], ib.at[r], i_send.at[d], i_recv.at[r], row_dev((r + d) % nr))

    for d in range(1, nr):
        i_copy(d).start()
    for d in range(1, nr):
        k = (r + d) % nr
        remote(ib.at[k], ib.at[k], i_send.at[d], i_recv.at[k], row_dev(k)).wait_recv()
    for k in range(nr):
        image_ref[:, k * chunk:(k + 1) * chunk] = ib[k]

    for place in range(line):
        hops(place, lambda copy: copy.wait_send())
    for d in range(1, n):
        ss_copy(d).wait_send()
        pg_copy(d).wait_send()
        part_copy((c + d) % n).wait_send()
    for d in range(1, nr):
        gx_copy(d).wait_send()
        u_copy(d).wait_send()
        i_copy(d).wait_send()


def solution(mesh):
    n, nr = mesh.shape["col"], mesh.shape["row"]

    def body(row_coords, col_coords, start_block):
        _, block_rows, atoms = row_coords.shape
        cols, vecs = start_block.shape
        local = n * block_rows
        chunk = cols // nr
        dma = pltpu.SemaphoreType.DMA
        basis, image = pl.pallas_call(
            functools.partial(kernel, n, nr, local * nr, cols * n),
            out_shape=(
                jax.ShapeDtypeStruct((vecs, local), F32),
                jax.ShapeDtypeStruct((vecs, cols), F32),
            ),
            in_specs=[pl.BlockSpec(memory_space=pltpu.VMEM)] * 3,
            out_specs=[pl.BlockSpec(memory_space=pltpu.VMEM)] * 2,
            scratch_shapes=[
                pltpu.VMEM((n, 3, block_rows, atoms), BF16),
                pltpu.VMEM((3, cols, atoms), BF16),
                pltpu.VMEM((8, cols), F32),
                pltpu.VMEM((block_rows, 128), F32),
                pltpu.VMEM((3 * block_rows, atoms), BF16),
                pltpu.VMEM((3, 3 * block_rows, TILE), F32),
                pltpu.VMEM((3, 3 * block_rows, TILE), F32),
                pltpu.VMEM((local, cols), BF16),
                pltpu.VMEM((local, cols), BF16),
                pltpu.VMEM((2 * vecs + 16, cols), BF16),
                pltpu.VMEM((n, 8, vecs), F32),
                pltpu.VMEM((n, vecs + 8, block_rows), F32),
                pltpu.VMEM((n, vecs + 8, block_rows), F32),
                pltpu.VMEM((n, vecs + 8, block_rows), F32),
                pltpu.VMEM((vecs + 8, local), F32),
                pltpu.VMEM((2 * vecs + 16, local), BF16),
                pltpu.VMEM((nr, vecs, 256), F32),
                pltpu.VMEM((nr, vecs + 8, chunk), F32),
                pltpu.VMEM((nr, vecs + 8, chunk), F32),
                pltpu.VMEM((nr, vecs, chunk), F32),
                dma((3, n)), dma((n,)), dma((n,)), dma((n,)), dma((n,)), dma((n,)), dma((n,)), dma((n,)),
                dma((nr,)), dma((nr,)), dma((nr,)), dma((nr,)), dma((nr,)), dma((nr,)),
            ],
            compiler_params=pltpu.CompilerParams(
                collective_id=0, has_side_effects=True, vmem_limit_bytes=48 * 1024 * 1024
            ),
        )(row_coords, col_coords, start_block.T)
        return (basis.T, image.T)

    in_specs = (P(None, ("row", "col"), None), P(None, "col", None), P("col", None))
    out_specs = (P("row", None), P("col", None))
    return jax.shard_map(body, mesh=mesh, in_specs=in_specs, out_specs=out_specs, check_vma=False)
```

```python
import functools
import math

import jax
import jax.numpy as jnp
from jax import lax
from jax.experimental import pallas as pl
from jax.experimental.pallas import tpu as pltpu
from jax.sharding import PartitionSpec as P

NEWTON = 8
TILE = 256
MESH = pl.DeviceIdType.MESH
HIGHEST = lax.Precision.HIGHEST
F32, BF16 = jnp.float32, jnp.bfloat16


def dot_nt(left, right, precision=None):
    return lax.dot_general(
        left, right, (((1,), (1,)), ((), ())), precision=precision, preferred_element_type=F32
    )


def dot_nn(left, right, precision=None):
    return lax.dot_general(
        left, right, (((1,), (0,)), ((), ())), precision=precision, preferred_element_type=F32
    )


def split(value):
    high = value.astype(BF16)
    return high, (value - high.astype(F32)).astype(BF16)


def setup_terms(s):
    c00 = s[1][1] * s[2][2] - s[1][2] * s[2][1]
    c01 = s[1][2] * s[2][0] - s[1][0] * s[2][2]
    c02 = s[1][0] * s[2][1] - s[1][1] * s[2][0]
    c10 = s[2][1] * s[0][2] - s[2][2] * s[0][1]
    c11 = s[2][2] * s[0][0] - s[2][0] * s[0][2]
    c12 = s[2][0] * s[0][1] - s[2][1] * s[0][0]
    c20 = s[0][1] * s[1][2] - s[0][2] * s[1][1]
    c21 = s[0][2] * s[1][0] - s[0][0] * s[1][2]
    c22 = s[0][0] * s[1][1] - s[0][1] * s[1][0]
    det = s[0][0] * c00 + s[0][1] * c01 + s[0][2] * c02
    square = lambda items: functools.reduce(lambda a, b: a + b, [v * v for v in items])
    total = square([s[a][b] for a in range(3) for b in range(3)])
    cof = square([c00, c01, c02, c10, c11, c12, c20, c21, c22])
    return total, cof, -2.0 * det


def newton(coeffs, lam):
    total, cof, g = coeffs
    m = lam * lam - total
    value = 0.25 * (m * m) + (g * lam - cof)
    return lam - value * pl.reciprocal(m * lam + g, approx=True)


def kernel(n, nr, total_rows, total_cols, row_hbm, col_hbm, st_hbm, basis_ref, image_ref,
           st_ref, rbuf, rraw, cc, cn_ref, rn_ref, s_a, s_b, d_hi, d_lo, lhs, ssb, pout, part, agb, q_ref, lhs2,
           gx, uout, ub, ib,
           in_sem, ag_send, ag_recv, ss_send, ss_recv, pa_send, pa_recv, pg_send, pg_recv,
           gx_send, gx_recv, u_send, u_recv, i_send, i_recv):
    c, r = lax.axis_index("col"), lax.axis_index("row")
    line = n // 2
    z, x = c // 2, c % 2
    _, block_rows, atoms = row_hbm.shape
    cols = col_hbm.shape[1]
    vecs = st_hbm.shape[0]
    chunk = cols // nr
    tiles = cols // TILE

    def col_dev(k):
        return (r, k)

    def row_dev(k):
        return (k, c)

    def remote(src, dst, send, recv, dev):
        return pltpu.make_async_remote_copy(
            src_ref=src, dst_ref=dst, send_sem=send, recv_sem=recv, device_id=dev, device_id_type=MESH
        )

    loads = [
        pltpu.make_async_copy(row_hbm, rraw, in_sem.at[0]),
        pltpu.make_async_copy(col_hbm, cc, in_sem.at[1]),
        pltpu.make_async_copy(st_hbm, st_ref, in_sem.at[2]),
    ]
    for load in loads:
        load.start()

    barrier = pltpu.get_barrier_semaphore()
    for d in range(1, n):
        pl.semaphore_signal(barrier, inc=1, device_id=col_dev((c + d) % n), device_id_type=MESH)
    for d in range(1, nr):
        pl.semaphore_signal(barrier, inc=1, device_id=row_dev((r + d) % nr), device_id_type=MESH)
    loads[0].wait()
    for a in range(3):
        v = rraw[a].astype(F32)
        v = (v - jnp.sum(v, axis=1, keepdims=True) * (1.0 / atoms)).astype(BF16).astype(F32)
        rbuf[c, a] = (v * (1.0 / atoms)).astype(BF16)
    pl.semaphore_wait(barrier, n - 1 + nr - 1)

    def hop(block, way):
        dev = col_dev((c + 1 - 2 * x, c + 2, c - 2)[way])
        return remote(rbuf.at[block], rbuf.at[block], ag_send.at[way, block], ag_recv.at[block], dev)

    def hops(block_z, act):
        block = block_z * 2 + x
        act(hop(block, 0))

        @pl.when((block_z <= z) & (z < line - 1))
        def _():
            act(hop(block, 1))

        @pl.when((block_z >= z) & (z > 0))
        def _():
            act(hop(block, 2))

    hops(z, lambda copy: copy.start())

    loads[2].wait()
    st = st_ref[...]
    st_hi, st_lo = split(st)
    lhs[0:vecs, :] = st_hi
    lhs[vecs:2 * vecs, :] = st_lo
    lhs[2 * vecs:2 * vecs + 16, :] = jnp.ones((16, cols), BF16)
    ssb[c] = dot_nt(jnp.ones((8, cols), F32), st, HIGHEST)

    def ss_copy(d):
        k = (c + d) % n
        return remote(ssb.at[c], ssb.at[c], ss_send.at[d], ss_recv.at[c], col_dev(k))

    for d in range(1, n):
        ss_copy(d).start()

    loads[1].wait()
    step_rows = 128

    def centre_cols(k, carry):
        at = pl.ds(pl.multiple_of(k * step_rows, step_rows), step_rows)
        squares = jnp.zeros((step_rows, atoms), F32)
        for b in range(3):
            v = cc[b, at, :].astype(F32)
            v = (v - jnp.sum(v, axis=1, keepdims=True) * (1.0 / atoms)).astype(BF16)
            cc[b, at, :] = v
            v = v.astype(F32)
            squares = squares + v * v
        cn_ref[:, at] = dot_nt(jnp.ones((8, atoms), F32), squares, HIGHEST) * (0.5 / atoms)
        return carry

    lax.fori_loop(0, cols // step_rows, centre_cols, 0)

    near = jnp.minimum(z, line - 1 - z)
    sign = jnp.where(z < line - 1 - z, 1, -1)

    def line_place(q):
        both = jnp.where(q % 2 == 1, (q + 1) // 2, -(q // 2))
        return z + jnp.where(q <= 2 * near, both, sign * (q - near))

    def part_copy(block):
        return remote(pout.at[block], part.at[c], pa_send.at[block], pa_recv.at[c], col_dev(block))

    def block_at(p):
        return line_place(p // 2) * 2 + jnp.where(p % 2 == 1, 1 - x, x)

    def norms(block, slot):
        squares = jnp.zeros((block_rows, atoms), F32)
        for a in range(3):
            v = rbuf[block, a].astype(F32)
            squares = squares + v * v
        norm = jnp.sum(squares, axis=1, keepdims=True) * (0.5 * atoms)
        rn_ref[slot] = jnp.broadcast_to(norm, (block_rows, 128))

    def cross(block, t, out):
        at = pl.ds(pl.multiple_of(t * TILE, TILE), TILE)
        rows = rbuf[block].reshape(3 * block_rows, atoms)
        for b in range(3):
            out[b] = dot_nt(rows, cc[b, at, :])

    groups = [
        [(i, l) for i in range(i0, i0 + 32, 8) for l in range(0, TILE, 128)]
        for i0 in range(0, block_rows, 32)
    ]

    def solve_pair(block, slot, t, between):
        def half(tile, i, l):
            cn = cn_ref[:, pl.ds(pl.multiple_of(tile * TILE + l, 128), 128)]
            return rn_ref[slot, i:i + 8, :] + cn

        def coeffs(src, i, l):
            at = [slice(a * block_rows + i, a * block_rows + i + 8) for a in range(3)]
            return setup_terms([[src[b, at[a], l:l + 128] for b in range(3)] for a in range(3)])

        stream = [(t, s_a, g) for g in groups] + [(t + 1, s_b, g) for g in groups]
        ready = [coeffs(s_a, i, l) for i, l in groups[0]]
        for index, (tile, _, group) in enumerate(stream):
            after = stream[index + 1] if index + 1 < len(stream) else None
            lam = [half(tile, i, l) for i, l in group]
            upcoming = []
            for step in range(NEWTON):
                lam = [newton(ready[k], lam[k]) for k in range(len(group))]
                if after is not None and step < len(after[2]):
                    upcoming.append(coeffs(after[1], *after[2][step]))
            if index == len(groups) - 1:
                between()
            dist = {place: half(tile, *place) - v for place, v in zip(group, lam)}
            for i, l in group:
                if i % 16 == 0:
                    value = jnp.concatenate([dist[(i, l)], dist[(i + 8, l)]], axis=0)
                    at_rows = pl.ds(pl.multiple_of(block * block_rows + i, 16), 16)
                    at_cols = pl.ds(pl.multiple_of(tile * TILE + l, 128), 128)
                    high, low = split(value)
                    d_hi[at_rows, at_cols] = high
                    d_lo[at_rows, at_cols] = low
            ready = upcoming

    def run_block(p, carry):
        block = block_at(p)
        coming = block_at(jnp.minimum(p + 1, n - 1))
        slot = p % 2

        @pl.when((p % 2 == 1) & (p < n - 1))
        def _():
            far = (p + 1) // 2
            for place in (z + far, z - far):
                @pl.when((place >= 0) & (place < line))
                def _():
                    hop(place * 2 + x, 0).wait_recv()
                    hops(place, lambda copy: copy.start())

        def pair(k, inner):
            t = 2 * k
            last = k == tiles // 2 - 1

            @pl.when(last & (p < n - 1))
            def _():
                @pl.when(p % 2 == 0)
                def _():
                    hop(coming, 0).wait_recv()

                norms(coming, 1 - slot)

            cross(block, t + 1, s_b)
            solve_pair(
                block, slot, t,
                lambda: cross(jnp.where(last, coming, block), jnp.where(last, 0, t + 2), s_a),
            )
            return inner

        lax.fori_loop(0, tiles // 2, pair, 0)

        at = pl.ds(pl.multiple_of(block * block_rows, block_rows), block_rows)
        high = dot_nt(lhs[...], d_hi[at, :])
        low = dot_nt(lhs[...], d_lo[at, :])
        both = high + low
        pout[block, 0:vecs] = both[0:vecs] + both[vecs:2 * vecs]
        pout[block, vecs:vecs + 8] = both[2 * vecs:2 * vecs + 8]

        @pl.when(block == c)
        def _():
            part[c] = pout[block]

        @pl.when(block != c)
        def _():
            part_copy(block).start()

        return carry

    norms(c, 0)
    cross(c, 0, s_a)
    lax.fori_loop(0, n, run_block, 0)

    for d in range(1, n):
        k = (c + d) % n
        remote(ssb.at[k], ssb.at[k], ss_send.at[d], ss_recv.at[k], col_dev(k)).wait_recv()
        remote(pout.at[k], part.at[k], pa_send.at[k], pa_recv.at[k], col_dev(k)).wait_recv()
    summed, starts = part[0], ssb[0]
    for k in range(1, n):
        summed, starts = summed + part[k], starts + ssb[k]
    eye = lax.broadcasted_iota(jnp.int32, (vecs, vecs), 0) == lax.broadcasted_iota(jnp.int32, (vecs, vecs), 1)
    mean = jnp.sum(jnp.where(eye, jnp.broadcast_to(starts[0:1, :], (vecs, vecs)), 0.0), axis=1, keepdims=True)
    mean = mean * (1.0 / total_cols)
    agb[c, 0:vecs] = summed[0:vecs] - mean * summed[vecs:vecs + 1]
    agb[c, vecs:vecs + 8] = summed[vecs:vecs + 8]

    def pg_copy(d):
        return remote(agb.at[c], agb.at[c], pg_send.at[d], pg_recv.at[c], col_dev((c + d) % n))

    for d in range(1, n):
        pg_copy(d).start()
    for d in range(1, n):
        k = (c + d) % n
        remote(agb.at[k], agb.at[k], pg_send.at[d], pg_recv.at[k], col_dev(k)).wait_recv()

    local = n * block_rows
    for k in range(n):
        q_ref[:, k * block_rows:(k + 1) * block_rows] = agb[k]
    prod = q_ref[0:vecs, :]
    row_total = q_ref[vecs:vecs + 1, :]
    local_mean = jnp.sum(prod, axis=1, keepdims=True) * (1.0 / local)
    q = prod - local_mean
    q_ref[0:vecs, :] = q
    q_hi, q_lo = split(q)
    lhs2[0:vecs, :] = q_hi
    lhs2[vecs:2 * vecs, :] = q_lo
    lhs2[2 * vecs:2 * vecs + 16, :] = jnp.ones((16, local), BF16)
    gx[r, :, 0:vecs] = dot_nt(q, q, HIGHEST)
    lane = lax.broadcasted_iota(jnp.int32, (vecs, 128), 1)
    extra = jnp.where(lane == 0, local_mean, 0.0)
    extra = extra + jnp.where(lane == 1, jnp.sum(q * row_total, axis=1, keepdims=True), 0.0)
    extra = extra + jnp.where(lane == 2, jnp.sum(row_total, axis=1, keepdims=True), 0.0)
    gx[r, :, 128:256] = extra

    def gx_copy(d):
        return remote(gx.at[r], gx.at[r], gx_send.at[d], gx_recv.at[r], row_dev((r + d) % nr))

    for d in range(1, nr):
        gx_copy(d).start()

    def u_copy(d):
        o = (r + d) % nr
        return remote(uout.at[d], ub.at[r], u_send.at[d], u_recv.at[r], row_dev(o))

    for d in list(range(1, nr)) + [0]:
        o = (r + d) % nr
        at = pl.ds(pl.multiple_of(o * chunk, chunk), chunk)
        high = dot_nn(lhs2[...], d_hi[:, at])
        both = high + dot_nn(lhs2[...], d_lo[:, at])
        product = both[0:vecs] + both[vecs:2 * vecs]
        sums = both[2 * vecs:2 * vecs + 8]
        if d:
            uout[d, 0:vecs] = product
            uout[d, vecs:vecs + 8] = sums
            u_copy(d).start()
        else:
            ub[r, 0:vecs] = product
            ub[r, vecs:vecs + 8] = sums

    for d in range(1, nr):
        k = (r + d) % nr
        remote(gx.at[k], gx.at[k], gx_send.at[d], gx_recv.at[k], row_dev(k)).wait_recv()
    means = [gx[k, :, 128:129] for k in range(nr)]
    mean = sum(means) * (1.0 / nr)
    shift = jnp.zeros((vecs, 128), F32)
    gram = jnp.zeros((vecs, vecs), F32)
    weighted = jnp.zeros((vecs, 1), F32)
    for k in range(nr):
        gram = gram + gx[k, :, 0:vecs]
        shift = shift + jnp.where(lane == k, means[k] - mean, 0.0)
        weighted = weighted + gx[k, :, 129:130] + (means[k] - mean) * gx[k, :, 130:131]
    gram = (gram + float(local) * dot_nt(shift, shift, HIGHEST)) * (1.0 / total_rows)

    work = jnp.concatenate([gram, jnp.where(eye, 1.0, 0.0)], axis=1)
    below = lax.broadcasted_iota(jnp.int32, (vecs, 1), 0)
    pivots = jnp.zeros((vecs, 1), F32)
    for k in range(vecs):
        top = work[k:k + 1, :]
        pivot = top[:, k:k + 1]
        pivots = jnp.where(below == k, pivot, pivots)
        factor = jnp.where(below > k, work[:, k:k + 1], 0.0)
        work = work - factor * (top * (1.0 / pivot))
    inverse = work[:, vecs:2 * vecs] * lax.rsqrt(pivots)

    own_mean = jnp.sum(jnp.where(lane == r, shift, 0.0), axis=1, keepdims=True)
    basis_ref[...] = -dot_nn(inverse, q_ref[0:vecs, :] + own_mean, HIGHEST)

    for d in range(1, nr):
        k = (r + d) % nr
        remote(uout.at[d], ub.at[k], u_send.at[d], u_recv.at[k], row_dev(k)).wait_recv()
    gathered = jnp.broadcast_to(weighted * (-1.0 / total_cols), (vecs, chunk))
    for k in range(nr):
        gathered = gathered + (ub[k, 0:vecs] + (means[k] - mean) * ub[k, vecs:vecs + 1])
    ib[r] = dot_nn(inverse, gathered, HIGHEST) * (1.0 / math.sqrt(total_rows))

    def i_copy(d):
        return remote(ib.at[r], ib.at[r], i_send.at[d], i_recv.at[r], row_dev((r + d) % nr))

    for d in range(1, nr):
        i_copy(d).start()
    for d in range(1, nr):
        k = (r + d) % nr
        remote(ib.at[k], ib.at[k], i_send.at[d], i_recv.at[k], row_dev(k)).wait_recv()
    for k in range(nr):
        image_ref[:, k * chunk:(k + 1) * chunk] = ib[k]

    for place in range(line):
        hops(place, lambda copy: copy.wait_send())
    for d in range(1, n):
        ss_copy(d).wait_send()
        pg_copy(d).wait_send()
        part_copy((c + d) % n).wait_send()
    for d in range(1, nr):
        gx_copy(d).wait_send()
        u_copy(d).wait_send()
        i_copy(d).wait_send()


def solution(mesh):
    n, nr = mesh.shape["col"], mesh.shape["row"]

    def body(row_coords, col_coords, start_block):
        _, block_rows, atoms = row_coords.shape
        cols, vecs = start_block.shape
        local = n * block_rows
        chunk = cols // nr
        dma = pltpu.SemaphoreType.DMA
        basis, image = pl.pallas_call(
            functools.partial(kernel, n, nr, local * nr, cols * n),
            out_shape=(
                jax.ShapeDtypeStruct((vecs, local), F32),
                jax.ShapeDtypeStruct((vecs, cols), F32),
            ),
            in_specs=[pl.BlockSpec(memory_space=pl.ANY)] * 3,
            out_specs=[pl.BlockSpec(memory_space=pltpu.VMEM)] * 2,
            scratch_shapes=[
                pltpu.VMEM((vecs, cols), F32),
                pltpu.VMEM((n, 3, block_rows, atoms), BF16),
                pltpu.VMEM((3, block_rows, atoms), BF16),
                pltpu.VMEM((3, cols, atoms), BF16),
                pltpu.VMEM((8, cols), F32),
                pltpu.VMEM((2, block_rows, 128), F32),
                pltpu.VMEM((3, 3 * block_rows, TILE), F32),
                pltpu.VMEM((3, 3 * block_rows, TILE), F32),
                pltpu.VMEM((local, cols), BF16),
                pltpu.VMEM((local, cols), BF16),
                pltpu.VMEM((2 * vecs + 16, cols), BF16),
                pltpu.VMEM((n, 8, vecs), F32),
                pltpu.VMEM((n, vecs + 8, block_rows), F32),
                pltpu.VMEM((n, vecs + 8, block_rows), F32),
                pltpu.VMEM((n, vecs + 8, block_rows), F32),
                pltpu.VMEM((vecs + 8, local), F32),
                pltpu.VMEM((2 * vecs + 16, local), BF16),
                pltpu.VMEM((nr, vecs, 256), F32),
                pltpu.VMEM((nr, vecs + 8, chunk), F32),
                pltpu.VMEM((nr, vecs + 8, chunk), F32),
                pltpu.VMEM((nr, vecs, chunk), F32),
                dma((3,)), dma((3, n)), dma((n,)), dma((n,)), dma((n,)), dma((n,)), dma((n,)), dma((n,)), dma((n,)),
                dma((nr,)), dma((nr,)), dma((nr,)), dma((nr,)), dma((nr,)), dma((nr,)),
            ],
            compiler_params=pltpu.CompilerParams(
                collective_id=0, has_side_effects=True, vmem_limit_bytes=56 * 1024 * 1024
            ),
        )(row_coords, col_coords, start_block.T)
        return (basis.T, image.T)

    in_specs = (P(None, ("row", "col"), None), P(None, "col", None), P("col", None))
    out_specs = (P("row", None), P("col", None))
    return jax.shard_map(body, mesh=mesh, in_specs=in_specs, out_specs=out_specs, check_vma=False)
```

```python
import functools
import math

import jax
import jax.numpy as jnp
from jax import lax
from jax.experimental import pallas as pl
from jax.experimental.pallas import tpu as pltpu
from jax.sharding import PartitionSpec as P

NEWTON = 8
TILE = 256
MESH = pl.DeviceIdType.MESH
HIGHEST = lax.Precision.HIGHEST
F32, BF16 = jnp.float32, jnp.bfloat16


def dot_nt(left, right, precision=None):
    return lax.dot_general(
        left, right, (((1,), (1,)), ((), ())), precision=precision, preferred_element_type=F32
    )


def dot_nn(left, right, precision=None):
    return lax.dot_general(
        left, right, (((1,), (0,)), ((), ())), precision=precision, preferred_element_type=F32
    )


def split(value):
    high = value.astype(BF16)
    return high, (value - high.astype(F32)).astype(BF16)


def setup_terms(s):
    c00 = s[1][1] * s[2][2] - s[1][2] * s[2][1]
    c01 = s[1][2] * s[2][0] - s[1][0] * s[2][2]
    c02 = s[1][0] * s[2][1] - s[1][1] * s[2][0]
    c10 = s[2][1] * s[0][2] - s[2][2] * s[0][1]
    c11 = s[2][2] * s[0][0] - s[2][0] * s[0][2]
    c12 = s[2][0] * s[0][1] - s[2][1] * s[0][0]
    c20 = s[0][1] * s[1][2] - s[0][2] * s[1][1]
    c21 = s[0][2] * s[1][0] - s[0][0] * s[1][2]
    c22 = s[0][0] * s[1][1] - s[0][1] * s[1][0]
    det = s[0][0] * c00 + s[0][1] * c01 + s[0][2] * c02
    square = lambda items: functools.reduce(lambda a, b: a + b, [v * v for v in items])
    total = square([s[a][b] for a in range(3) for b in range(3)])
    cof = square([c00, c01, c02, c10, c11, c12, c20, c21, c22])
    return total, cof, -2.0 * det


def newton(coeffs, lam):
    total, cof, g = coeffs
    m = lam * lam - total
    value = 0.25 * (m * m) + (g * lam - cof)
    return lam - value * pl.reciprocal(m * lam + g, approx=True)


def kernel(n, nr, total_rows, total_cols, row_hbm, col_hbm, st_hbm, basis_ref, image_ref,
           st_ref, rbuf, rraw, craw, cc, cn_ref, rn_ref, s_a, s_b, d_hi, d_lo, start, ssb, pout, part, agb, q_ref, lhs2,
           gx, uout, ub, ib,
           in_sem, ag_send, ag_recv, ss_send, ss_recv, pa_send, pa_recv, pg_send, pg_recv,
           gx_send, gx_recv, u_send, u_recv, i_send, i_recv):
    c, r = lax.axis_index("col"), lax.axis_index("row")
    line = n // 2
    z, x = c // 2, c % 2
    _, block_rows, atoms = row_hbm.shape
    cols = col_hbm.shape[1]
    vecs = st_hbm.shape[0]
    chunk = cols // nr
    tiles = cols // TILE

    def col_dev(k):
        return (r, k)

    def row_dev(k):
        return (k, c)

    def remote(src, dst, send, recv, dev):
        return pltpu.make_async_remote_copy(
            src_ref=src, dst_ref=dst, send_sem=send, recv_sem=recv, device_id=dev, device_id_type=MESH
        )

    loads = [
        pltpu.make_async_copy(row_hbm, rraw, in_sem.at[0]),
        pltpu.make_async_copy(col_hbm, craw, in_sem.at[1]),
        pltpu.make_async_copy(st_hbm, st_ref, in_sem.at[2]),
    ]
    for load in loads:
        load.start()

    barrier = pltpu.get_barrier_semaphore()
    for d in range(1, n):
        pl.semaphore_signal(barrier, inc=1, device_id=col_dev((c + d) % n), device_id_type=MESH)
    for d in range(1, nr):
        pl.semaphore_signal(barrier, inc=1, device_id=row_dev((r + d) % nr), device_id_type=MESH)
    loads[0].wait()
    for a in range(3):
        v = rraw[a].astype(F32)
        v = (v - jnp.sum(v, axis=1, keepdims=True) * (1.0 / atoms)).astype(BF16).astype(F32)
        rbuf[c, a] = (v * (1.0 / atoms)).astype(BF16)
    pl.semaphore_wait(barrier, n - 1 + nr - 1)

    def hop(block, way):
        dev = col_dev((c + 1 - 2 * x, c + 2, c - 2)[way])
        return remote(rbuf.at[block], rbuf.at[block], ag_send.at[way, block], ag_recv.at[block], dev)

    def hops(block_z, act):
        block = block_z * 2 + x
        act(hop(block, 0))

        @pl.when((block_z <= z) & (z < line - 1))
        def _():
            act(hop(block, 1))

        @pl.when((block_z >= z) & (z > 0))
        def _():
            act(hop(block, 2))

    hops(z, lambda copy: copy.start())

    loads[2].wait()
    st = st_ref[...].T
    st_hi, st_lo = split(st)
    start[:, 0:vecs] = st_hi
    start[:, vecs:2 * vecs] = st_lo
    start[:, 2 * vecs:] = jnp.ones((cols, 128), BF16)
    ssb[c] = jnp.broadcast_to(jnp.sum(st, axis=0, keepdims=True), (8, vecs))

    def ss_copy(d):
        k = (c + d) % n
        return remote(ssb.at[c], ssb.at[c], ss_send.at[d], ss_recv.at[c], col_dev(k))

    for d in range(1, n):
        ss_copy(d).start()

    loads[1].wait()
    step_rows = 128

    def centre_cols(k, carry):
        at = pl.ds(pl.multiple_of(k * step_rows, step_rows), step_rows)
        squares = jnp.zeros((atoms, step_rows), F32)
        for b in range(3):
            v = craw[b, at, :].astype(F32)
            v = v - jnp.sum(v, axis=1, keepdims=True) * (1.0 / atoms)
            v = v.T.astype(BF16)
            cc[b, :, at] = v
            v = v.astype(F32)
            squares = squares + v * v
        norm = jnp.sum(squares, axis=0, keepdims=True) * (0.5 / atoms)
        cn_ref[:, at] = jnp.broadcast_to(norm, (8, step_rows))
        return carry

    lax.fori_loop(0, cols // step_rows, centre_cols, 0)

    near = jnp.minimum(z, line - 1 - z)
    sign = jnp.where(z < line - 1 - z, 1, -1)

    def line_place(q):
        both = jnp.where(q % 2 == 1, (q + 1) // 2, -(q // 2))
        return z + jnp.where(q <= 2 * near, both, sign * (q - near))

    def part_copy(block):
        return remote(pout.at[block], part.at[c], pa_send.at[block], pa_recv.at[c], col_dev(block))

    def block_at(p):
        return line_place(p // 2) * 2 + jnp.where(p % 2 == 1, 1 - x, x)

    def norms(block, slot):
        squares = jnp.zeros((block_rows, atoms), F32)
        for a in range(3):
            v = rbuf[block, a].astype(F32)
            squares = squares + v * v
        norm = jnp.sum(squares, axis=1, keepdims=True) * (0.5 * atoms)
        rn_ref[slot] = jnp.broadcast_to(norm, (block_rows, 128))

    def cross(block, t, out):
        at = pl.ds(pl.multiple_of(t * TILE, TILE), TILE)
        rows = rbuf[block].reshape(3 * block_rows, atoms)
        for b in range(3):
            out[b] = dot_nn(rows, cc[b, :, at])

    groups = [
        [(i, l) for i in range(i0, i0 + 32, 8) for l in range(0, TILE, 128)]
        for i0 in range(0, block_rows, 32)
    ]

    def solve_pair(block, slot, t, between):
        def half(tile, i, l):
            cn = cn_ref[:, pl.ds(pl.multiple_of(tile * TILE + l, 128), 128)]
            return rn_ref[slot, i:i + 8, :] + cn

        def coeffs(src, i, l):
            at = [slice(a * block_rows + i, a * block_rows + i + 8) for a in range(3)]
            return setup_terms([[src[b, at[a], l:l + 128] for b in range(3)] for a in range(3)])

        stream = [(t, s_a, g) for g in groups] + [(t + 1, s_b, g) for g in groups]
        ready = [coeffs(s_a, i, l) for i, l in groups[0]]
        for index, (tile, _, group) in enumerate(stream):
            after = stream[index + 1] if index + 1 < len(stream) else None
            lam = [half(tile, i, l) for i, l in group]
            upcoming = []
            for step in range(NEWTON):
                lam = [newton(ready[k], lam[k]) for k in range(len(group))]
                if after is not None and step < len(after[2]):
                    upcoming.append(coeffs(after[1], *after[2][step]))
            if index == len(groups) - 1:
                between()
            dist = {place: half(tile, *place) - v for place, v in zip(group, lam)}
            for i, l in group:
                if i % 16 == 0:
                    value = jnp.concatenate([dist[(i, l)], dist[(i + 8, l)]], axis=0)
                    at_rows = pl.ds(pl.multiple_of(block * block_rows + i, 16), 16)
                    at_cols = pl.ds(pl.multiple_of(tile * TILE + l, 128), 128)
                    high, low = split(value)
                    d_hi[at_rows, at_cols] = high
                    d_lo[at_rows, at_cols] = low
            ready = upcoming

    def run_block(p, carry):
        block = block_at(p)
        coming = block_at(jnp.minimum(p + 1, n - 1))
        slot = p % 2

        @pl.when((p % 2 == 1) & (p < n - 1))
        def _():
            far = (p + 1) // 2
            for place in (z + far, z - far):
                @pl.when((place >= 0) & (place < line))
                def _():
                    hop(place * 2 + x, 0).wait_recv()
                    hops(place, lambda copy: copy.start())

        def pair(k, inner):
            t = 2 * k
            last = k == tiles // 2 - 1

            @pl.when(last & (p < n - 1))
            def _():
                @pl.when(p % 2 == 0)
                def _():
                    hop(coming, 0).wait_recv()

                norms(coming, 1 - slot)

            cross(block, t + 1, s_b)
            solve_pair(
                block, slot, t,
                lambda: cross(jnp.where(last, coming, block), jnp.where(last, 0, t + 2), s_a),
            )
            return inner

        lax.fori_loop(0, tiles // 2, pair, 0)

        at = pl.ds(pl.multiple_of(block * block_rows, block_rows), block_rows)
        both = (dot_nn(d_hi[at, :], start[...]) + dot_nn(d_lo[at, :], start[...])).T
        pout[block, 0:vecs] = both[0:vecs] + both[vecs:2 * vecs]
        pout[block, vecs:vecs + 8] = both[2 * vecs:2 * vecs + 8]

        @pl.when(block == c)
        def _():
            part[c] = pout[block]

        @pl.when(block != c)
        def _():
            part_copy(block).start()

        return carry

    norms(c, 0)
    cross(c, 0, s_a)
    lax.fori_loop(0, n, run_block, 0)

    for d in range(1, n):
        k = (c + d) % n
        remote(ssb.at[k], ssb.at[k], ss_send.at[d], ss_recv.at[k], col_dev(k)).wait_recv()
        remote(pout.at[k], part.at[k], pa_send.at[k], pa_recv.at[k], col_dev(k)).wait_recv()
    summed, starts = part[0], ssb[0]
    for k in range(1, n):
        summed, starts = summed + part[k], starts + ssb[k]
    eye = lax.broadcasted_iota(jnp.int32, (vecs, vecs), 0) == lax.broadcasted_iota(jnp.int32, (vecs, vecs), 1)
    mean = jnp.sum(jnp.where(eye, jnp.broadcast_to(starts[0:1, :], (vecs, vecs)), 0.0), axis=1, keepdims=True)
    mean = mean * (1.0 / total_cols)
    agb[c, 0:vecs] = summed[0:vecs] - mean * summed[vecs:vecs + 1]
    agb[c, vecs:vecs + 8] = summed[vecs:vecs + 8]

    def pg_copy(d):
        return remote(agb.at[c], agb.at[c], pg_send.at[d], pg_recv.at[c], col_dev((c + d) % n))

    for d in range(1, n):
        pg_copy(d).start()
    for d in range(1, n):
        k = (c + d) % n
        remote(agb.at[k], agb.at[k], pg_send.at[d], pg_recv.at[k], col_dev(k)).wait_recv()

    local = n * block_rows
    for k in range(n):
        q_ref[:, k * block_rows:(k + 1) * block_rows] = agb[k]
    prod = q_ref[0:vecs, :]
    row_total = q_ref[vecs:vecs + 1, :]
    local_mean = jnp.sum(prod, axis=1, keepdims=True) * (1.0 / local)
    q = prod - local_mean
    q_ref[0:vecs, :] = q
    q_hi, q_lo = split(q)
    lhs2[0:vecs, :] = q_hi
    lhs2[vecs:2 * vecs, :] = q_lo
    lhs2[2 * vecs:2 * vecs + 16, :] = jnp.ones((16, local), BF16)
    gx[r, :, 0:vecs] = dot_nt(q, q, HIGHEST)
    lane = lax.broadcasted_iota(jnp.int32, (vecs, 128), 1)
    extra = jnp.where(lane == 0, local_mean, 0.0)
    extra = extra + jnp.where(lane == 1, jnp.sum(q * row_total, axis=1, keepdims=True), 0.0)
    extra = extra + jnp.where(lane == 2, jnp.sum(row_total, axis=1, keepdims=True), 0.0)
    gx[r, :, 128:256] = extra

    def gx_copy(d):
        return remote(gx.at[r], gx.at[r], gx_send.at[d], gx_recv.at[r], row_dev((r + d) % nr))

    for d in range(1, nr):
        gx_copy(d).start()

    def u_copy(d):
        o = (r + d) % nr
        return remote(uout.at[d], ub.at[r], u_send.at[d], u_recv.at[r], row_dev(o))

    for d in list(range(1, nr)) + [0]:
        o = (r + d) % nr
        at = pl.ds(pl.multiple_of(o * chunk, chunk), chunk)
        high = dot_nn(lhs2[...], d_hi[:, at])
        both = high + dot_nn(lhs2[...], d_lo[:, at])
        product = both[0:vecs] + both[vecs:2 * vecs]
        sums = both[2 * vecs:2 * vecs + 8]
        if d:
            uout[d, 0:vecs] = product
            uout[d, vecs:vecs + 8] = sums
            u_copy(d).start()
        else:
            ub[r, 0:vecs] = product
            ub[r, vecs:vecs + 8] = sums

    for d in range(1, nr):
        k = (r + d) % nr
        remote(gx.at[k], gx.at[k], gx_send.at[d], gx_recv.at[k], row_dev(k)).wait_recv()
    means = [gx[k, :, 128:129] for k in range(nr)]
    mean = sum(means) * (1.0 / nr)
    shift = jnp.zeros((vecs, 128), F32)
    gram = jnp.zeros((vecs, vecs), F32)
    weighted = jnp.zeros((vecs, 1), F32)
    for k in range(nr):
        gram = gram + gx[k, :, 0:vecs]
        shift = shift + jnp.where(lane == k, means[k] - mean, 0.0)
        weighted = weighted + gx[k, :, 129:130] + (means[k] - mean) * gx[k, :, 130:131]
    gram = (gram + float(local) * dot_nt(shift, shift, HIGHEST)) * (1.0 / total_rows)

    work = jnp.concatenate([gram, jnp.where(eye, 1.0, 0.0)], axis=1)
    below = lax.broadcasted_iota(jnp.int32, (vecs, 1), 0)
    pivots = jnp.zeros((vecs, 1), F32)
    for k in range(vecs):
        top = work[k:k + 1, :]
        pivot = top[:, k:k + 1]
        pivots = jnp.where(below == k, pivot, pivots)
        factor = jnp.where(below > k, work[:, k:k + 1], 0.0)
        work = work - factor * (top * (1.0 / pivot))
    inverse = work[:, vecs:2 * vecs] * lax.rsqrt(pivots)

    own_mean = jnp.sum(jnp.where(lane == r, shift, 0.0), axis=1, keepdims=True)
    basis_ref[...] = -dot_nn(inverse, q_ref[0:vecs, :] + own_mean, HIGHEST)

    for d in range(1, nr):
        k = (r + d) % nr
        remote(uout.at[d], ub.at[k], u_send.at[d], u_recv.at[k], row_dev(k)).wait_recv()
    gathered = jnp.broadcast_to(weighted * (-1.0 / total_cols), (vecs, chunk))
    for k in range(nr):
        gathered = gathered + (ub[k, 0:vecs] + (means[k] - mean) * ub[k, vecs:vecs + 1])
    ib[r] = dot_nn(inverse, gathered, HIGHEST) * (1.0 / math.sqrt(total_rows))

    def i_copy(d):
        return remote(ib.at[r], ib.at[r], i_send.at[d], i_recv.at[r], row_dev((r + d) % nr))

    for d in range(1, nr):
        i_copy(d).start()
    for d in range(1, nr):
        k = (r + d) % nr
        remote(ib.at[k], ib.at[k], i_send.at[d], i_recv.at[k], row_dev(k)).wait_recv()
    for k in range(nr):
        image_ref[:, k * chunk:(k + 1) * chunk] = ib[k]

    for place in range(line):
        hops(place, lambda copy: copy.wait_send())
    for d in range(1, n):
        ss_copy(d).wait_send()
        pg_copy(d).wait_send()
        part_copy((c + d) % n).wait_send()
    for d in range(1, nr):
        gx_copy(d).wait_send()
        u_copy(d).wait_send()
        i_copy(d).wait_send()


def solution(mesh):
    n, nr = mesh.shape["col"], mesh.shape["row"]

    def body(row_coords, col_coords, start_block):
        _, block_rows, atoms = row_coords.shape
        cols, vecs = start_block.shape
        local = n * block_rows
        chunk = cols // nr
        dma = pltpu.SemaphoreType.DMA
        basis, image = pl.pallas_call(
            functools.partial(kernel, n, nr, local * nr, cols * n),
            out_shape=(
                jax.ShapeDtypeStruct((vecs, local), F32),
                jax.ShapeDtypeStruct((vecs, cols), F32),
            ),
            in_specs=[pl.BlockSpec(memory_space=pltpu.HBM)] * 3,
            out_specs=[pl.BlockSpec(memory_space=pltpu.VMEM)] * 2,
            scratch_shapes=[
                pltpu.VMEM((vecs, cols), F32),
                pltpu.VMEM((n, 3, block_rows, atoms), BF16),
                pltpu.VMEM((3, block_rows, atoms), BF16),
                pltpu.VMEM((3, cols, atoms), BF16),
                pltpu.VMEM((3, atoms, cols), BF16),
                pltpu.VMEM((8, cols), F32),
                pltpu.VMEM((2, block_rows, 128), F32),
                pltpu.VMEM((3, 3 * block_rows, TILE), F32),
                pltpu.VMEM((3, 3 * block_rows, TILE), F32),
                pltpu.VMEM((local, cols), BF16),
                pltpu.VMEM((local, cols), BF16),
                pltpu.VMEM((cols, 2 * vecs + 128), BF16),
                pltpu.VMEM((n, 8, vecs), F32),
                pltpu.VMEM((n, vecs + 8, block_rows), F32),
                pltpu.VMEM((n, vecs + 8, block_rows), F32),
                pltpu.VMEM((n, vecs + 8, block_rows), F32),
                pltpu.VMEM((vecs + 8, local), F32),
                pltpu.VMEM((2 * vecs + 16, local), BF16),
                pltpu.VMEM((nr, vecs, 256), F32),
                pltpu.VMEM((nr, vecs + 8, chunk), F32),
                pltpu.VMEM((nr, vecs + 8, chunk), F32),
                pltpu.VMEM((nr, vecs, chunk), F32),
                dma((3,)), dma((3, n)), dma((n,)), dma((n,)), dma((n,)), dma((n,)), dma((n,)), dma((n,)), dma((n,)),
                dma((nr,)), dma((nr,)), dma((nr,)), dma((nr,)), dma((nr,)), dma((nr,)),
            ],
            compiler_params=pltpu.CompilerParams(
                collective_id=0, has_side_effects=True, vmem_limit_bytes=54500 * 1024
            ),
        )(row_coords, col_coords, start_block.T)
        return (basis.T, image.T)

    in_specs = (P(None, ("row", "col"), None), P(None, "col", None), P("col", None))
    out_specs = (P("row", None), P("col", None))
    return jax.shard_map(body, mesh=mesh, in_specs=in_specs, out_specs=out_specs, check_vma=False)
```

```python
import functools
import math

import jax
import jax.numpy as jnp
from jax import lax
from jax.experimental import pallas as pl
from jax.experimental.pallas import tpu as pltpu
from jax.sharding import PartitionSpec as P

NEWTON = 8
TILE = 256
MESH = pl.DeviceIdType.MESH
HIGHEST = lax.Precision.HIGHEST
F32, BF16 = jnp.float32, jnp.bfloat16


def dot_nt(left, right, precision=None):
    return lax.dot_general(
        left, right, (((1,), (1,)), ((), ())), precision=precision, preferred_element_type=F32
    )


def dot_nn(left, right, precision=None):
    return lax.dot_general(
        left, right, (((1,), (0,)), ((), ())), precision=precision, preferred_element_type=F32
    )


def split(value):
    high = value.astype(BF16)
    return high, (value - high.astype(F32)).astype(BF16)


def setup_terms(s):
    c00 = s[1][1] * s[2][2] - s[1][2] * s[2][1]
    c01 = s[1][2] * s[2][0] - s[1][0] * s[2][2]
    c02 = s[1][0] * s[2][1] - s[1][1] * s[2][0]
    c10 = s[2][1] * s[0][2] - s[2][2] * s[0][1]
    c11 = s[2][2] * s[0][0] - s[2][0] * s[0][2]
    c12 = s[2][0] * s[0][1] - s[2][1] * s[0][0]
    c20 = s[0][1] * s[1][2] - s[0][2] * s[1][1]
    c21 = s[0][2] * s[1][0] - s[0][0] * s[1][2]
    c22 = s[0][0] * s[1][1] - s[0][1] * s[1][0]
    det = s[0][0] * c00 + s[0][1] * c01 + s[0][2] * c02
    square = lambda items: functools.reduce(lambda a, b: a + b, [v * v for v in items])
    total = square([s[a][b] for a in range(3) for b in range(3)])
    cof = square([c00, c01, c02, c10, c11, c12, c20, c21, c22])
    return total, cof, -2.0 * det


def newton(coeffs, lam):
    total, cof, g = coeffs
    m = lam * lam - total
    value = 0.25 * (m * m) + (g * lam - cof)
    return lam - value * pl.reciprocal(m * lam + g, approx=True)


def kernel(n, nr, total_rows, total_cols, row_hbm, col_hbm, st_hbm, basis_ref, image_ref,
           st_ref, rbuf, rraw, craw, cc, cn_ref, rn_ref, s_a, s_b, d_hi, d_lo, start, ssb, pout, part, agb, q_ref, lhs2,
           gx, uout, ub, ib,
           in_sem, ag_send, ag_recv, ss_send, ss_recv, pa_send, pa_recv, pg_send, pg_recv,
           gx_send, gx_recv, u_send, u_recv, i_send, i_recv):
    c, r = lax.axis_index("col"), lax.axis_index("row")
    line = n // 2
    z, x = c // 2, c % 2
    _, block_rows, atoms = row_hbm.shape
    cols = col_hbm.shape[1]
    vecs = st_hbm.shape[0]
    chunk = cols // nr
    tiles = cols // TILE

    def col_dev(k):
        return (r, k)

    def row_dev(k):
        return (k, c)

    def remote(src, dst, send, recv, dev):
        return pltpu.make_async_remote_copy(
            src_ref=src, dst_ref=dst, send_sem=send, recv_sem=recv, device_id=dev, device_id_type=MESH
        )

    loads = [
        pltpu.make_async_copy(row_hbm, rraw, in_sem.at[0]),
        pltpu.make_async_copy(col_hbm, craw, in_sem.at[1]),
        pltpu.make_async_copy(st_hbm, st_ref, in_sem.at[2]),
    ]
    for load in loads:
        load.start()

    barrier = pltpu.get_barrier_semaphore()
    for d in range(1, n):
        pl.semaphore_signal(barrier, inc=1, device_id=col_dev((c + d) % n), device_id_type=MESH)
    for d in range(1, nr):
        pl.semaphore_signal(barrier, inc=1, device_id=row_dev((r + d) % nr), device_id_type=MESH)
    loads[0].wait()
    for a in range(3):
        v = rraw[a].astype(F32)
        v = (v - jnp.sum(v, axis=1, keepdims=True) * (1.0 / atoms)).astype(BF16).astype(F32)
        rbuf[c, a] = (v * (1.0 / atoms)).astype(BF16)
    pl.semaphore_wait(barrier, n - 1 + nr - 1)

    half_rows = block_rows // 2

    def hop(block, half, way):
        dev = col_dev((c + 1 - 2 * x, c + 2, c - 2)[way])
        piece = rbuf.at[block, :, half * half_rows:(half + 1) * half_rows, :]
        return remote(piece, piece, ag_send.at[way, half, block], ag_recv.at[half, block], dev)

    def is_end(place):
        return (place == 0) | (place == line - 1)

    def line_hops(block, place, half, act):
        @pl.when((place <= z) & (z < line - 1))
        def _():
            act(hop(block, half, 1))

        @pl.when((place >= z) & (z > 0))
        def _():
            act(hop(block, half, 2))

    def hops(place, act):
        block = place * 2 + x
        for half in range(2):
            line_hops(block, place, half, act)
        act(hop(block, 0, 0))

        @pl.when(jnp.logical_not(is_end(place)) | (place == z))
        def _():
            act(hop(block, 1, 0))

    def crossed_hops(place, act):
        line_hops(place * 2 + 1 - x, place, 1, act)

    start_copy = lambda copy: copy.start()
    hops(z, start_copy)

    loads[2].wait()
    st = st_ref[...].T
    st_hi, st_lo = split(st)
    start[:, 0:vecs] = st_hi
    start[:, vecs:2 * vecs] = st_lo
    start[:, 2 * vecs:] = jnp.ones((cols, 128), BF16)
    ssb[c] = jnp.broadcast_to(jnp.sum(st, axis=0, keepdims=True), (8, vecs))

    def ss_copy(d):
        k = (c + d) % n
        return remote(ssb.at[c], ssb.at[c], ss_send.at[d], ss_recv.at[c], col_dev(k))

    for d in range(1, n):
        ss_copy(d).start()

    loads[1].wait()
    step_rows = 128

    def centre_cols(k, carry):
        at = pl.ds(pl.multiple_of(k * step_rows, step_rows), step_rows)
        squares = jnp.zeros((atoms, step_rows), F32)
        for b in range(3):
            v = craw[b, at, :].astype(F32)
            v = v - jnp.sum(v, axis=1, keepdims=True) * (1.0 / atoms)
            v = v.T.astype(BF16)
            cc[b, :, at] = v
            v = v.astype(F32)
            squares = squares + v * v
        norm = jnp.sum(squares, axis=0, keepdims=True) * (0.5 / atoms)
        cn_ref[:, at] = jnp.broadcast_to(norm, (8, step_rows))
        return carry

    lax.fori_loop(0, cols // step_rows, centre_cols, 0)

    near = jnp.minimum(z, line - 1 - z)
    sign = jnp.where(z < line - 1 - z, 1, -1)

    def line_place(q):
        both = jnp.where(q % 2 == 1, (q + 1) // 2, -(q // 2))
        return z + jnp.where(q <= 2 * near, both, sign * (q - near))

    def part_copy(block):
        return remote(pout.at[block], part.at[c], pa_send.at[block], pa_recv.at[c], col_dev(block))

    def block_at(p):
        return line_place(p // 2) * 2 + jnp.where(p % 2 == 1, 1 - x, x)

    def norms(block, slot):
        squares = jnp.zeros((block_rows, atoms), F32)
        for a in range(3):
            v = rbuf[block, a].astype(F32)
            squares = squares + v * v
        norm = jnp.sum(squares, axis=1, keepdims=True) * (0.5 * atoms)
        rn_ref[slot] = jnp.broadcast_to(norm, (block_rows, 128))

    def cross(block, t, out):
        at = pl.ds(pl.multiple_of(t * TILE, TILE), TILE)
        rows = rbuf[block].reshape(3 * block_rows, atoms)
        for b in range(3):
            out[b] = dot_nn(rows, cc[b, :, at])

    groups = [
        [(i, l) for i in range(i0, i0 + 32, 8) for l in range(0, TILE, 128)]
        for i0 in range(0, block_rows, 32)
    ]

    def solve_pair(block, slot, t, between):
        def half(tile, i, l):
            cn = cn_ref[:, pl.ds(pl.multiple_of(tile * TILE + l, 128), 128)]
            return rn_ref[slot, i:i + 8, :] + cn

        def coeffs(src, i, l):
            at = [slice(a * block_rows + i, a * block_rows + i + 8) for a in range(3)]
            return setup_terms([[src[b, at[a], l:l + 128] for b in range(3)] for a in range(3)])

        stream = [(t, s_a, g) for g in groups] + [(t + 1, s_b, g) for g in groups]
        ready = [coeffs(s_a, i, l) for i, l in groups[0]]
        for index, (tile, _, group) in enumerate(stream):
            after = stream[index + 1] if index + 1 < len(stream) else None
            lam = [half(tile, i, l) for i, l in group]
            upcoming = []
            for step in range(NEWTON):
                lam = [newton(ready[k], lam[k]) for k in range(len(group))]
                if after is not None and step < len(after[2]):
                    upcoming.append(coeffs(after[1], *after[2][step]))
            if index == len(groups) - 1:
                between()
            dist = {place: half(tile, *place) - v for place, v in zip(group, lam)}
            for i, l in group:
                if i % 16 == 0:
                    value = jnp.concatenate([dist[(i, l)], dist[(i + 8, l)]], axis=0)
                    at_rows = pl.ds(pl.multiple_of(block * block_rows + i, 16), 16)
                    at_cols = pl.ds(pl.multiple_of(tile * TILE + l, 128), 128)
                    high, low = split(value)
                    d_hi[at_rows, at_cols] = high
                    d_lo[at_rows, at_cols] = low
            ready = upcoming

    def run_block(p, carry):
        block = block_at(p)
        coming = block_at(jnp.minimum(p + 1, n - 1))
        slot = p % 2

        def fetch():
            far = p // 2 + 1

            @pl.when((p % 2 == 0) & (far < line))
            def _():
                for place in (z + far, z - far):
                    @pl.when((place >= 0) & (place < line))
                    def _():
                        hop(place * 2 + x, 0, 0).wait_recv()
                        hop(place * 2 + x, 1, 0).wait_recv()
                        hops(place, start_copy)

            @pl.when(p % 2 == 0)
            def _():
                place = line_place(p // 2)
                hop(coming, 0, 0).wait_recv()

                @pl.when(jnp.logical_not(is_end(place)) | (place == z))
                def _():
                    hop(coming, 1, 0).wait_recv()

                @pl.when(is_end(place) & (place == z))
                def _():
                    crossed_hops(place, start_copy)

            @pl.when((p % 2 == 1) & (far < line))
            def _():
                for place, end in ((z + far, line - 1), (z - far, 0)):
                    @pl.when(place == end)
                    def _():
                        hop(place * 2 + 1 - x, 1, 0).wait_recv()
                        crossed_hops(place, start_copy)

        def pair(k, inner):
            t = 2 * k
            last = k == tiles // 2 - 1

            @pl.when(last & (p < n - 1))
            def _():
                fetch()
                norms(coming, 1 - slot)

            cross(block, t + 1, s_b)
            solve_pair(
                block, slot, t,
                lambda: cross(jnp.where(last, coming, block), jnp.where(last, 0, t + 2), s_a),
            )
            return inner

        lax.fori_loop(0, tiles // 2, pair, 0)

        at = pl.ds(pl.multiple_of(block * block_rows, block_rows), block_rows)
        both = (dot_nn(d_hi[at, :], start[...]) + dot_nn(d_lo[at, :], start[...])).T
        pout[block, 0:vecs] = both[0:vecs] + both[vecs:2 * vecs]
        pout[block, vecs:vecs + 8] = both[2 * vecs:2 * vecs + 8]

        @pl.when(block == c)
        def _():
            part[c] = pout[block]

        @pl.when(block != c)
        def _():
            part_copy(block).start()

        return carry

    norms(c, 0)
    cross(c, 0, s_a)
    lax.fori_loop(0, n, run_block, 0)

    for d in range(1, n):
        k = (c + d) % n
        remote(ssb.at[k], ssb.at[k], ss_send.at[d], ss_recv.at[k], col_dev(k)).wait_recv()
        remote(pout.at[k], part.at[k], pa_send.at[k], pa_recv.at[k], col_dev(k)).wait_recv()
    summed, starts = part[0], ssb[0]
    for k in range(1, n):
        summed, starts = summed + part[k], starts + ssb[k]
    eye = lax.broadcasted_iota(jnp.int32, (vecs, vecs), 0) == lax.broadcasted_iota(jnp.int32, (vecs, vecs), 1)
    mean = jnp.sum(jnp.where(eye, jnp.broadcast_to(starts[0:1, :], (vecs, vecs)), 0.0), axis=1, keepdims=True)
    mean = mean * (1.0 / total_cols)
    agb[c, 0:vecs] = summed[0:vecs] - mean * summed[vecs:vecs + 1]
    agb[c, vecs:vecs + 8] = summed[vecs:vecs + 8]

    def pg_copy(d):
        return remote(agb.at[c], agb.at[c], pg_send.at[d], pg_recv.at[c], col_dev((c + d) % n))

    for d in range(1, n):
        pg_copy(d).start()
    for d in range(1, n):
        k = (c + d) % n
        remote(agb.at[k], agb.at[k], pg_send.at[d], pg_recv.at[k], col_dev(k)).wait_recv()

    local = n * block_rows
    for k in range(n):
        q_ref[:, k * block_rows:(k + 1) * block_rows] = agb[k]
    prod = q_ref[0:vecs, :]
    row_total = q_ref[vecs:vecs + 1, :]
    local_mean = jnp.sum(prod, axis=1, keepdims=True) * (1.0 / local)
    q = prod - local_mean
    q_ref[0:vecs, :] = q
    q_hi, q_lo = split(q)
    lhs2[0:vecs, :] = q_hi
    lhs2[vecs:2 * vecs, :] = q_lo
    lhs2[2 * vecs:2 * vecs + 16, :] = jnp.ones((16, local), BF16)
    gx[r, :, 0:vecs] = dot_nt(q, q, HIGHEST)
    lane = lax.broadcasted_iota(jnp.int32, (vecs, 128), 1)
    extra = jnp.where(lane == 0, local_mean, 0.0)
    extra = extra + jnp.where(lane == 1, jnp.sum(q * row_total, axis=1, keepdims=True), 0.0)
    extra = extra + jnp.where(lane == 2, jnp.sum(row_total, axis=1, keepdims=True), 0.0)
    gx[r, :, 128:256] = extra

    def gx_copy(d):
        return remote(gx.at[r], gx.at[r], gx_send.at[d], gx_recv.at[r], row_dev((r + d) % nr))

    for d in range(1, nr):
        gx_copy(d).start()

    def u_copy(d):
        o = (r + d) % nr
        return remote(uout.at[d], ub.at[r], u_send.at[d], u_recv.at[r], row_dev(o))

    for d in list(range(1, nr)) + [0]:
        o = (r + d) % nr
        at = pl.ds(pl.multiple_of(o * chunk, chunk), chunk)
        high = dot_nn(lhs2[...], d_hi[:, at])
        both = high + dot_nn(lhs2[...], d_lo[:, at])
        product = both[0:vecs] + both[vecs:2 * vecs]
        sums = both[2 * vecs:2 * vecs + 8]
        if d:
            uout[d, 0:vecs] = product
            uout[d, vecs:vecs + 8] = sums
            u_copy(d).start()
        else:
            ub[r, 0:vecs] = product
            ub[r, vecs:vecs + 8] = sums

    for d in range(1, nr):
        k = (r + d) % nr
        remote(gx.at[k], gx.at[k], gx_send.at[d], gx_recv.at[k], row_dev(k)).wait_recv()
    means = [gx[k, :, 128:129] for k in range(nr)]
    mean = sum(means) * (1.0 / nr)
    shift = jnp.zeros((vecs, 128), F32)
    gram = jnp.zeros((vecs, vecs), F32)
    weighted = jnp.zeros((vecs, 1), F32)
    for k in range(nr):
        gram = gram + gx[k, :, 0:vecs]
        shift = shift + jnp.where(lane == k, means[k] - mean, 0.0)
        weighted = weighted + gx[k, :, 129:130] + (means[k] - mean) * gx[k, :, 130:131]
    gram = (gram + float(local) * dot_nt(shift, shift, HIGHEST)) * (1.0 / total_rows)

    work = jnp.concatenate([gram, jnp.where(eye, 1.0, 0.0)], axis=1)
    below = lax.broadcasted_iota(jnp.int32, (vecs, 1), 0)
    ratio, scale = jnp.zeros((vecs, 1), F32), jnp.zeros((vecs, 1), F32)
    for k in range(0, vecs, 2):
        top, low = work[k:k + 1, :], work[k + 1:k + 2, :]
        left, right = work[:, k:k + 1], work[:, k + 1:k + 2]
        first, off, second = top[:, k:k + 1], top[:, k + 1:k + 2], low[:, k + 1:k + 2]
        inv = 1.0 / (first * second - off * off)
        ratio = jnp.where(below == k + 1, off / first, ratio)
        scale = jnp.where(below == k, first, jnp.where(below == k + 1, second - off * (off / first), scale))
        keep = jnp.where(below > k + 1, inv, 0.0)
        work = work - ((left * second - right * off) * keep) * top - ((right * first - left * off) * keep) * low
    unit = work[:, vecs:2 * vecs]
    above = jnp.concatenate([unit[vecs - 1:vecs, :], unit[0:vecs - 1, :]], axis=0)
    inverse = (unit - ratio * above) * lax.rsqrt(scale)

    own_mean = jnp.sum(jnp.where(lane == r, shift, 0.0), axis=1, keepdims=True)
    basis_ref[...] = -dot_nn(inverse, q_ref[0:vecs, :] + own_mean, HIGHEST)

    for d in range(1, nr):
        k = (r + d) % nr
        remote(uout.at[d], ub.at[k], u_send.at[d], u_recv.at[k], row_dev(k)).wait_recv()
    gathered = jnp.broadcast_to(weighted * (-1.0 / total_cols), (vecs, chunk))
    for k in range(nr):
        gathered = gathered + (ub[k, 0:vecs] + (means[k] - mean) * ub[k, vecs:vecs + 1])
    ib[r] = dot_nn(inverse, gathered, HIGHEST) * (1.0 / math.sqrt(total_rows))

    def i_copy(d):
        return remote(ib.at[r], ib.at[r], i_send.at[d], i_recv.at[r], row_dev((r + d) % nr))

    for d in range(1, nr):
        i_copy(d).start()
    for d in range(1, nr):
        k = (r + d) % nr
        remote(ib.at[k], ib.at[k], i_send.at[d], i_recv.at[k], row_dev(k)).wait_recv()
    for k in range(nr):
        image_ref[:, k * chunk:(k + 1) * chunk] = ib[k]

    for place in range(line):
        hops(place, lambda copy: copy.wait_send())
    for place in (0, line - 1):
        crossed_hops(place, lambda copy: copy.wait_send())
    for d in range(1, n):
        ss_copy(d).wait_send()
        pg_copy(d).wait_send()
        part_copy((c + d) % n).wait_send()
    for d in range(1, nr):
        gx_copy(d).wait_send()
        u_copy(d).wait_send()
        i_copy(d).wait_send()


def solution(mesh):
    n, nr = mesh.shape["col"], mesh.shape["row"]

    def body(row_coords, col_coords, start_block):
        _, block_rows, atoms = row_coords.shape
        cols, vecs = start_block.shape
        local = n * block_rows
        chunk = cols // nr
        dma = pltpu.SemaphoreType.DMA
        basis, image = pl.pallas_call(
            functools.partial(kernel, n, nr, local * nr, cols * n),
            out_shape=(
                jax.ShapeDtypeStruct((vecs, local), F32),
                jax.ShapeDtypeStruct((vecs, cols), F32),
            ),
            in_specs=[pl.BlockSpec(memory_space=pltpu.HBM)] * 3,
            out_specs=[pl.BlockSpec(memory_space=pltpu.VMEM)] * 2,
            scratch_shapes=[
                pltpu.VMEM((vecs, cols), F32),
                pltpu.VMEM((n, 3, block_rows, atoms), BF16),
                pltpu.VMEM((3, block_rows, atoms), BF16),
                pltpu.VMEM((3, cols, atoms), BF16),
                pltpu.VMEM((3, atoms, cols), BF16),
                pltpu.VMEM((8, cols), F32),
                pltpu.VMEM((2, block_rows, 128), F32),
                pltpu.VMEM((3, 3 * block_rows, TILE), F32),
                pltpu.VMEM((3, 3 * block_rows, TILE), F32),
                pltpu.VMEM((local, cols), BF16),
                pltpu.VMEM((local, cols), BF16),
                pltpu.VMEM((cols, 2 * vecs + 128), BF16),
                pltpu.VMEM((n, 8, vecs), F32),
                pltpu.VMEM((n, vecs + 8, block_rows), F32),
                pltpu.VMEM((n, vecs + 8, block_rows), F32),
                pltpu.VMEM((n, vecs + 8, block_rows), F32),
                pltpu.VMEM((vecs + 8, local), F32),
                pltpu.VMEM((2 * vecs + 16, local), BF16),
                pltpu.VMEM((nr, vecs, 256), F32),
                pltpu.VMEM((nr, vecs + 8, chunk), F32),
                pltpu.VMEM((nr, vecs + 8, chunk), F32),
                pltpu.VMEM((nr, vecs, chunk), F32),
                dma((3,)), dma((3, 2, n)), dma((2, n)), dma((n,)), dma((n,)), dma((n,)), dma((n,)), dma((n,)), dma((n,)),
                dma((nr,)), dma((nr,)), dma((nr,)), dma((nr,)), dma((nr,)), dma((nr,)),
            ],
            compiler_params=pltpu.CompilerParams(
                collective_id=0, has_side_effects=True, vmem_limit_bytes=54500 * 1024
            ),
        )(row_coords, col_coords, start_block.T)
        return (basis.T, image.T)

    in_specs = (P(None, ("row", "col"), None), P(None, "col", None), P("col", None))
    out_specs = (P("row", None), P("col", None))
    return jax.shard_map(body, mesh=mesh, in_specs=in_specs, out_specs=out_specs, check_vma=False)
```

```python
import functools
import math

import jax
import jax.numpy as jnp
from jax import lax
from jax.experimental import pallas as pl
from jax.experimental.pallas import tpu as pltpu
from jax.sharding import PartitionSpec as P

NEWTON = 8
TILE = 256
MESH = pl.DeviceIdType.MESH
HIGHEST = lax.Precision.HIGHEST
F32, BF16 = jnp.float32, jnp.bfloat16


def dot_nt(left, right, precision=None):
    return lax.dot_general(
        left, right, (((1,), (1,)), ((), ())), precision=precision, preferred_element_type=F32
    )


def dot_nn(left, right, precision=None):
    return lax.dot_general(
        left, right, (((1,), (0,)), ((), ())), precision=precision, preferred_element_type=F32
    )


def split(value):
    high = value.astype(BF16)
    return high, (value - high.astype(F32)).astype(BF16)


def setup_terms(s):
    c00 = s[1][1] * s[2][2] - s[1][2] * s[2][1]
    c01 = s[1][2] * s[2][0] - s[1][0] * s[2][2]
    c02 = s[1][0] * s[2][1] - s[1][1] * s[2][0]
    c10 = s[2][1] * s[0][2] - s[2][2] * s[0][1]
    c11 = s[2][2] * s[0][0] - s[2][0] * s[0][2]
    c12 = s[2][0] * s[0][1] - s[2][1] * s[0][0]
    c20 = s[0][1] * s[1][2] - s[0][2] * s[1][1]
    c21 = s[0][2] * s[1][0] - s[0][0] * s[1][2]
    c22 = s[0][0] * s[1][1] - s[0][1] * s[1][0]
    det = s[0][0] * c00 + s[0][1] * c01 + s[0][2] * c02
    square = lambda items: functools.reduce(lambda a, b: a + b, [v * v for v in items])
    total = square([s[a][b] for a in range(3) for b in range(3)])
    cof = square([c00, c01, c02, c10, c11, c12, c20, c21, c22])
    return total, cof, -2.0 * det


def newton(coeffs, lam, beside):
    every = range(len(lam))
    totals = [coeffs(0, k) for k in every]
    squares = [lam[k] * lam[k] for k in every]
    m = [squares[k] - totals[k] for k in every]
    g = [coeffs(2, k) for k in every]
    slope = [m[k] * lam[k] for k in every]
    slope = [slope[k] + g[k] for k in every]
    inverse = [pl.reciprocal(slope[k], approx=True) for k in every]
    linear = [g[k] * lam[k] for k in every]
    cof = [coeffs(1, k) for k in every]
    linear = [linear[k] - cof[k] for k in every]
    quarter = [0.25 * m[k] for k in every]
    value = [quarter[k] * m[k] for k in every]
    value = [value[k] + linear[k] for k in every]
    beside()
    step = [value[k] * inverse[k] for k in every]
    return [lam[k] - step[k] for k in every]


def kernel(n, nr, total_rows, total_cols, row_hbm, col_hbm, st_hbm, basis_ref, image_ref,
           st_ref, rbuf, rraw, craw, cc, cn_ref, rn_ref, co_ref, s_a, s_b, d_hi, d_lo, start, ssb, pout, part, agb, q_ref, lhs2,
           gx, uout, ub, ib,
           in_sem, ag_send, ag_recv, ss_send, ss_recv, pa_send, pa_recv, pg_send, pg_recv,
           gx_send, gx_recv, u_send, u_recv, i_send, i_recv):
    c, r = lax.axis_index("col"), lax.axis_index("row")
    line = n // 2
    z, x = c // 2, c % 2
    _, block_rows, atoms = row_hbm.shape
    cols = col_hbm.shape[1]
    vecs = st_hbm.shape[0]
    chunk = cols // nr
    tiles = cols // TILE

    def col_dev(k):
        return (r, k)

    def row_dev(k):
        return (k, c)

    def remote(src, dst, send, recv, dev):
        return pltpu.make_async_remote_copy(
            src_ref=src, dst_ref=dst, send_sem=send, recv_sem=recv, device_id=dev, device_id_type=MESH
        )

    loads = [
        pltpu.make_async_copy(row_hbm, rraw, in_sem.at[0]),
        pltpu.make_async_copy(col_hbm, craw, in_sem.at[1]),
        pltpu.make_async_copy(st_hbm, st_ref, in_sem.at[2]),
    ]
    for load in loads:
        load.start()

    barrier = pltpu.get_barrier_semaphore()
    for d in range(1, n):
        pl.semaphore_signal(barrier, inc=1, device_id=col_dev((c + d) % n), device_id_type=MESH)
    for d in range(1, nr):
        pl.semaphore_signal(barrier, inc=1, device_id=row_dev((r + d) % nr), device_id_type=MESH)
    loads[0].wait()
    for a in range(3):
        v = rraw[a].astype(F32)
        v = (v - jnp.sum(v, axis=1, keepdims=True) * (1.0 / atoms)).astype(BF16).astype(F32)
        rbuf[c, a] = (v * (1.0 / atoms)).astype(BF16)
    pl.semaphore_wait(barrier, n - 1 + nr - 1)

    half_rows = block_rows // 2

    def hop(block, half, way):
        dev = col_dev((c + 1 - 2 * x, c + 2, c - 2)[way])
        piece = rbuf.at[block, :, half * half_rows:(half + 1) * half_rows, :]
        return remote(piece, piece, ag_send.at[way, half, block], ag_recv.at[half, block], dev)

    def is_end(place):
        return (place == 0) | (place == line - 1)

    def line_hops(block, place, half, act):
        @pl.when((place <= z) & (z < line - 1))
        def _():
            act(hop(block, half, 1))

        @pl.when((place >= z) & (z > 0))
        def _():
            act(hop(block, half, 2))

    def hops(place, act):
        block = place * 2 + x
        for half in range(2):
            line_hops(block, place, half, act)
        act(hop(block, 0, 0))

        @pl.when(jnp.logical_not(is_end(place)) | (place == z))
        def _():
            act(hop(block, 1, 0))

    def crossed_hops(place, act):
        line_hops(place * 2 + 1 - x, place, 1, act)

    start_copy = lambda copy: copy.start()
    hops(z, start_copy)

    loads[2].wait()
    st = st_ref[...].T
    st_hi, st_lo = split(st)
    start[:, 0:vecs] = st_hi
    start[:, vecs:2 * vecs] = st_lo
    start[:, 2 * vecs:] = jnp.ones((cols, 128), BF16)
    ssb[c] = jnp.broadcast_to(jnp.sum(st, axis=0, keepdims=True), (8, vecs))

    def ss_copy(d):
        k = (c + d) % n
        return remote(ssb.at[c], ssb.at[c], ss_send.at[d], ss_recv.at[c], col_dev(k))

    for d in range(1, n):
        ss_copy(d).start()

    loads[1].wait()
    step_rows = 128

    def centre_cols(k, carry):
        at = pl.ds(pl.multiple_of(k * step_rows, step_rows), step_rows)
        squares = jnp.zeros((atoms, step_rows), F32)
        for b in range(3):
            v = craw[b, at, :].astype(F32)
            v = v - jnp.sum(v, axis=1, keepdims=True) * (1.0 / atoms)
            v = v.T.astype(BF16)
            cc[b, :, at] = v
            v = v.astype(F32)
            squares = squares + v * v
        norm = jnp.sum(squares, axis=0, keepdims=True) * (0.5 / atoms)
        cn_ref[:, at] = jnp.broadcast_to(norm, (8, step_rows))
        return carry

    lax.fori_loop(0, cols // step_rows, centre_cols, 0)

    near = jnp.minimum(z, line - 1 - z)
    sign = jnp.where(z < line - 1 - z, 1, -1)

    def line_place(q):
        both = jnp.where(q % 2 == 1, (q + 1) // 2, -(q // 2))
        return z + jnp.where(q <= 2 * near, both, sign * (q - near))

    def part_copy(block):
        return remote(pout.at[block], part.at[c], pa_send.at[block], pa_recv.at[c], col_dev(block))

    def block_at(p):
        return line_place(p // 2) * 2 + jnp.where(p % 2 == 1, 1 - x, x)

    def norms(block, slot):
        squares = jnp.zeros((block_rows, atoms), F32)
        for a in range(3):
            v = rbuf[block, a].astype(F32)
            squares = squares + v * v
        norm = jnp.sum(squares, axis=1, keepdims=True) * (0.5 * atoms)
        rn_ref[slot] = jnp.broadcast_to(norm, (block_rows, 128))

    def cross(block, t, out, parts=range(3)):
        at = pl.ds(pl.multiple_of(t * TILE, TILE), TILE)
        rows = rbuf[block].reshape(3 * block_rows, atoms)
        for b in parts:
            out[b] = dot_nn(rows, cc[b, :, at])

    groups = [
        [(i, l) for i in range(i0, i0 + 32, 8) for l in range(0, TILE, 128)]
        for i0 in range(0, block_rows, 32)
    ]

    def solve_pair(block, slot, t, coming, first):
        def half(tile, i, l):
            cn = cn_ref[:, pl.ds(pl.multiple_of(tile * TILE + l, 128), 128)]
            return rn_ref[slot, i:i + 8, :] + cn

        def coeffs(turn, k, src, i, l):
            at = [slice(a * block_rows + i, a * block_rows + i + 8) for a in range(3)]
            terms = setup_terms([[src[b, at[a], l:l + 128] for b in range(3)] for a in range(3)])
            for kind in range(3):
                co_ref[turn, kind, k] = terms[kind]

        stream = [(t, s_a, g) for g in groups] + [(t + 1, s_b, g) for g in groups]
        for k, (i, l) in enumerate(groups[0]):
            coeffs(0, k, s_a, i, l)
        for index, (tile, _, group) in enumerate(stream):
            after = stream[index + 1] if index + 1 < len(stream) else None
            turn = index % 2
            place = index % len(groups)
            if index < len(groups):
                if place < min(3, len(groups) - 1):
                    cross(block, t + 1, s_b, range(place, 3, max(1, min(3, len(groups) - 1))))
                elif len(groups) == 1:
                    cross(block, t + 1, s_b)
            elif place < min(3, len(groups)):
                cross(coming, first, s_a, range(place, 3, min(3, len(groups))))
            lam = [half(tile, i, l) for i, l in group]
            for step in range(NEWTON):

                def beside():
                    if after is not None and step < len(after[2]):
                        coeffs(1 - turn, step, after[1], *after[2][step])

                lam = newton(lambda kind, k: co_ref[turn, kind, k], lam, beside)
            dist = {place: half(tile, *place) - v for place, v in zip(group, lam)}
            for i, l in group:
                if i % 16 == 0:
                    value = jnp.concatenate([dist[(i, l)], dist[(i + 8, l)]], axis=0)
                    at_rows = pl.ds(pl.multiple_of(block * block_rows + i, 16), 16)
                    at_cols = pl.ds(pl.multiple_of(tile * TILE + l, 128), 128)
                    high, low = split(value)
                    d_hi[at_rows, at_cols] = high
                    d_lo[at_rows, at_cols] = low

    def run_block(p, carry):
        block = block_at(p)
        coming = block_at(jnp.minimum(p + 1, n - 1))
        slot = p % 2

        def fetch():
            far = p // 2 + 1

            @pl.when((p % 2 == 0) & (far < line))
            def _():
                for place in (z + far, z - far):
                    @pl.when((place >= 0) & (place < line))
                    def _():
                        hop(place * 2 + x, 0, 0).wait_recv()
                        hop(place * 2 + x, 1, 0).wait_recv()
                        hops(place, start_copy)

            @pl.when(p % 2 == 0)
            def _():
                place = line_place(p // 2)
                hop(coming, 0, 0).wait_recv()

                @pl.when(jnp.logical_not(is_end(place)) | (place == z))
                def _():
                    hop(coming, 1, 0).wait_recv()

                @pl.when(is_end(place) & (place == z))
                def _():
                    crossed_hops(place, start_copy)

            @pl.when((p % 2 == 1) & (far < line))
            def _():
                for place, end in ((z + far, line - 1), (z - far, 0)):
                    @pl.when(place == end)
                    def _():
                        hop(place * 2 + 1 - x, 1, 0).wait_recv()
                        crossed_hops(place, start_copy)

        def pair(k, inner):
            t = 2 * k
            last = k == tiles // 2 - 1

            @pl.when(last & (p < n - 1))
            def _():
                fetch()
                norms(coming, 1 - slot)

            solve_pair(block, slot, t, jnp.where(last, coming, block), jnp.where(last, 0, t + 2))
            return inner

        lax.fori_loop(0, tiles // 2, pair, 0)

        at = pl.ds(pl.multiple_of(block * block_rows, block_rows), block_rows)
        both = (dot_nn(d_hi[at, :], start[...]) + dot_nn(d_lo[at, :], start[...])).T
        pout[block, 0:vecs] = both[0:vecs] + both[vecs:2 * vecs]
        pout[block, vecs:vecs + 8] = both[2 * vecs:2 * vecs + 8]

        @pl.when(block == c)
        def _():
            part[c] = pout[block]

        @pl.when(block != c)
        def _():
            part_copy(block).start()

        return carry

    norms(c, 0)
    cross(c, 0, s_a)
    lax.fori_loop(0, n, run_block, 0)

    for d in range(1, n):
        k = (c + d) % n
        remote(ssb.at[k], ssb.at[k], ss_send.at[d], ss_recv.at[k], col_dev(k)).wait_recv()
        remote(pout.at[k], part.at[k], pa_send.at[k], pa_recv.at[k], col_dev(k)).wait_recv()
    summed, starts = part[0], ssb[0]
    for k in range(1, n):
        summed, starts = summed + part[k], starts + ssb[k]
    eye = lax.broadcasted_iota(jnp.int32, (vecs, vecs), 0) == lax.broadcasted_iota(jnp.int32, (vecs, vecs), 1)
    mean = jnp.sum(jnp.where(eye, jnp.broadcast_to(starts[0:1, :], (vecs, vecs)), 0.0), axis=1, keepdims=True)
    mean = mean * (1.0 / total_cols)
    agb[c, 0:vecs] = summed[0:vecs] - mean * summed[vecs:vecs + 1]
    agb[c, vecs:vecs + 8] = summed[vecs:vecs + 8]

    def pg_copy(d):
        return remote(agb.at[c], agb.at[c], pg_send.at[d], pg_recv.at[c], col_dev((c + d) % n))

    for d in range(1, n):
        pg_copy(d).start()
    for d in range(1, n):
        k = (c + d) % n
        remote(agb.at[k], agb.at[k], pg_send.at[d], pg_recv.at[k], col_dev(k)).wait_recv()

    local = n * block_rows
    for k in range(n):
        q_ref[:, k * block_rows:(k + 1) * block_rows] = agb[k]
    prod = q_ref[0:vecs, :]
    row_total = q_ref[vecs:vecs + 1, :]
    local_mean = jnp.sum(prod, axis=1, keepdims=True) * (1.0 / local)
    q = prod - local_mean
    q_ref[0:vecs, :] = q
    q_hi, q_lo = split(q)
    lhs2[0:vecs, :] = q_hi
    lhs2[vecs:2 * vecs, :] = q_lo
    lhs2[2 * vecs:2 * vecs + 16, :] = jnp.ones((16, local), BF16)
    gx[r, :, 0:vecs] = dot_nt(q, q, HIGHEST)
    lane = lax.broadcasted_iota(jnp.int32, (vecs, 128), 1)
    extra = jnp.where(lane == 0, local_mean, 0.0)
    extra = extra + jnp.where(lane == 1, jnp.sum(q * row_total, axis=1, keepdims=True), 0.0)
    extra = extra + jnp.where(lane == 2, jnp.sum(row_total, axis=1, keepdims=True), 0.0)
    gx[r, :, 128:256] = extra

    def gx_copy(d):
        return remote(gx.at[r], gx.at[r], gx_send.at[d], gx_recv.at[r], row_dev((r + d) % nr))

    for d in range(1, nr):
        gx_copy(d).start()

    def u_copy(d):
        o = (r + d) % nr
        return remote(uout.at[d], ub.at[r], u_send.at[d], u_recv.at[r], row_dev(o))

    for d in list(range(1, nr)) + [0]:
        o = (r + d) % nr
        at = pl.ds(pl.multiple_of(o * chunk, chunk), chunk)
        high = dot_nn(lhs2[...], d_hi[:, at])
        both = high + dot_nn(lhs2[...], d_lo[:, at])
        product = both[0:vecs] + both[vecs:2 * vecs]
        sums = both[2 * vecs:2 * vecs + 8]
        if d:
            uout[d, 0:vecs] = product
            uout[d, vecs:vecs + 8] = sums
            u_copy(d).start()
        else:
            ub[r, 0:vecs] = product
            ub[r, vecs:vecs + 8] = sums

    for d in range(1, nr):
        k = (r + d) % nr
        remote(gx.at[k], gx.at[k], gx_send.at[d], gx_recv.at[k], row_dev(k)).wait_recv()
    means = [gx[k, :, 128:129] for k in range(nr)]
    mean = sum(means) * (1.0 / nr)
    shift = jnp.zeros((vecs, 128), F32)
    gram = jnp.zeros((vecs, vecs), F32)
    weighted = jnp.zeros((vecs, 1), F32)
    for k in range(nr):
        gram = gram + gx[k, :, 0:vecs]
        shift = shift + jnp.where(lane == k, means[k] - mean, 0.0)
        weighted = weighted + gx[k, :, 129:130] + (means[k] - mean) * gx[k, :, 130:131]
    gram = (gram + float(local) * dot_nt(shift, shift, HIGHEST)) * (1.0 / total_rows)

    work = jnp.concatenate([gram, jnp.where(eye, 1.0, 0.0)], axis=1)
    below = lax.broadcasted_iota(jnp.int32, (vecs, 1), 0)
    ratio, scale = jnp.zeros((vecs, 1), F32), jnp.zeros((vecs, 1), F32)
    for k in range(0, vecs, 2):
        top, low = work[k:k + 1, :], work[k + 1:k + 2, :]
        left, right = work[:, k:k + 1], work[:, k + 1:k + 2]
        first, off, second = top[:, k:k + 1], top[:, k + 1:k + 2], low[:, k + 1:k + 2]
        inv = 1.0 / (first * second - off * off)
        ratio = jnp.where(below == k + 1, off / first, ratio)
        scale = jnp.where(below == k, first, jnp.where(below == k + 1, second - off * (off / first), scale))
        keep = jnp.where(below > k + 1, inv, 0.0)
        work = work - ((left * second - right * off) * keep) * top - ((right * first - left * off) * keep) * low
    unit = work[:, vecs:2 * vecs]
    above = jnp.concatenate([unit[vecs - 1:vecs, :], unit[0:vecs - 1, :]], axis=0)
    inverse = (unit - ratio * above) * lax.rsqrt(scale)

    own_mean = jnp.sum(jnp.where(lane == r, shift, 0.0), axis=1, keepdims=True)
    basis_ref[...] = -dot_nn(inverse, q_ref[0:vecs, :] + own_mean, HIGHEST)

    for d in range(1, nr):
        k = (r + d) % nr
        remote(uout.at[d], ub.at[k], u_send.at[d], u_recv.at[k], row_dev(k)).wait_recv()
    gathered = jnp.broadcast_to(weighted * (-1.0 / total_cols), (vecs, chunk))
    for k in range(nr):
        gathered = gathered + (ub[k, 0:vecs] + (means[k] - mean) * ub[k, vecs:vecs + 1])
    ib[r] = dot_nn(inverse, gathered, HIGHEST) * (1.0 / math.sqrt(total_rows))

    def i_copy(d):
        return remote(ib.at[r], ib.at[r], i_send.at[d], i_recv.at[r], row_dev((r + d) % nr))

    for d in range(1, nr):
        i_copy(d).start()
    for d in range(1, nr):
        k = (r + d) % nr
        remote(ib.at[k], ib.at[k], i_send.at[d], i_recv.at[k], row_dev(k)).wait_recv()
    for k in range(nr):
        image_ref[:, k * chunk:(k + 1) * chunk] = ib[k]

    for place in range(line):
        hops(place, lambda copy: copy.wait_send())
    for place in (0, line - 1):
        crossed_hops(place, lambda copy: copy.wait_send())
    for d in range(1, n):
        ss_copy(d).wait_send()
        pg_copy(d).wait_send()
        part_copy((c + d) % n).wait_send()
    for d in range(1, nr):
        gx_copy(d).wait_send()
        u_copy(d).wait_send()
        i_copy(d).wait_send()


def solution(mesh):
    n, nr = mesh.shape["col"], mesh.shape["row"]

    def body(row_coords, col_coords, start_block):
        _, block_rows, atoms = row_coords.shape
        cols, vecs = start_block.shape
        local = n * block_rows
        chunk = cols // nr
        dma = pltpu.SemaphoreType.DMA
        basis, image = pl.pallas_call(
            functools.partial(kernel, n, nr, local * nr, cols * n),
            out_shape=(
                jax.ShapeDtypeStruct((vecs, local), F32),
                jax.ShapeDtypeStruct((vecs, cols), F32),
            ),
            in_specs=[pl.BlockSpec(memory_space=pltpu.HBM)] * 3,
            out_specs=[pl.BlockSpec(memory_space=pltpu.VMEM)] * 2,
            scratch_shapes=[
                pltpu.VMEM((vecs, cols), F32),
                pltpu.VMEM((n, 3, block_rows, atoms), BF16),
                pltpu.VMEM((3, block_rows, atoms), BF16),
                pltpu.VMEM((3, cols, atoms), BF16),
                pltpu.VMEM((3, atoms, cols), BF16),
                pltpu.VMEM((8, cols), F32),
                pltpu.VMEM((2, block_rows, 128), F32),
                pltpu.VMEM((2, 3, 8, 8, 128), F32),
                pltpu.VMEM((3, 3 * block_rows, TILE), F32),
                pltpu.VMEM((3, 3 * block_rows, TILE), F32),
                pltpu.VMEM((local, cols), BF16),
                pltpu.VMEM((local, cols), BF16),
                pltpu.VMEM((cols, 2 * vecs + 128), BF16),
                pltpu.VMEM((n, 8, vecs), F32),
                pltpu.VMEM((n, vecs + 8, block_rows), F32),
                pltpu.VMEM((n, vecs + 8, block_rows), F32),
                pltpu.VMEM((n, vecs + 8, block_rows), F32),
                pltpu.VMEM((vecs + 8, local), F32),
                pltpu.VMEM((2 * vecs + 16, local), BF16),
                pltpu.VMEM((nr, vecs, 256), F32),
                pltpu.VMEM((nr, vecs + 8, chunk), F32),
                pltpu.VMEM((nr, vecs + 8, chunk), F32),
                pltpu.VMEM((nr, vecs, chunk), F32),
                dma((3,)), dma((3, 2, n)), dma((2, n)), dma((n,)), dma((n,)), dma((n,)), dma((n,)), dma((n,)), dma((n,)),
                dma((nr,)), dma((nr,)), dma((nr,)), dma((nr,)), dma((nr,)), dma((nr,)),
            ],
            compiler_params=pltpu.CompilerParams(
                collective_id=0, has_side_effects=True, vmem_limit_bytes=54500 * 1024
            ),
        )(row_coords, col_coords, start_block.T)
        return (basis.T, image.T)

    in_specs = (P(None, ("row", "col"), None), P(None, "col", None), P("col", None))
    out_specs = (P("row", None), P("col", None))
    return jax.shard_map(body, mesh=mesh, in_specs=in_specs, out_specs=out_specs, check_vma=False)
```

```python
import functools
import math

import jax
import jax.numpy as jnp
from jax import lax
from jax.experimental import pallas as pl
from jax.experimental.pallas import tpu as pltpu
from jax.sharding import PartitionSpec as P

NEWTON = 8
TILE = 256
MESH = pl.DeviceIdType.MESH
HIGHEST = lax.Precision.HIGHEST
F32, BF16 = jnp.float32, jnp.bfloat16


def dot_nt(left, right, precision=None):
    return lax.dot_general(
        left, right, (((1,), (1,)), ((), ())), precision=precision, preferred_element_type=F32
    )


def dot_nn(left, right, precision=None):
    return lax.dot_general(
        left, right, (((1,), (0,)), ((), ())), precision=precision, preferred_element_type=F32
    )


def split(value):
    high = value.astype(BF16)
    return high, (value - high.astype(F32)).astype(BF16)


def setup_terms(s):
    c00 = s[1][1] * s[2][2] - s[1][2] * s[2][1]
    c01 = s[1][2] * s[2][0] - s[1][0] * s[2][2]
    c02 = s[1][0] * s[2][1] - s[1][1] * s[2][0]
    c10 = s[2][1] * s[0][2] - s[2][2] * s[0][1]
    c11 = s[2][2] * s[0][0] - s[2][0] * s[0][2]
    c12 = s[2][0] * s[0][1] - s[2][1] * s[0][0]
    c20 = s[0][1] * s[1][2] - s[0][2] * s[1][1]
    c21 = s[0][2] * s[1][0] - s[0][0] * s[1][2]
    c22 = s[0][0] * s[1][1] - s[0][1] * s[1][0]
    det = s[0][0] * c00 + s[0][1] * c01 + s[0][2] * c02
    square = lambda items: functools.reduce(lambda a, b: a + b, [v * v for v in items])
    total = square([s[a][b] for a in range(3) for b in range(3)])
    cof = square([c00, c01, c02, c10, c11, c12, c20, c21, c22])
    return total, cof, -2.0 * det


def newton(coeffs, lam, beside):
    every = range(len(lam))
    totals = [coeffs(0, k) for k in every]
    squares = [lam[k] * lam[k] for k in every]
    m = [squares[k] - totals[k] for k in every]
    g = [coeffs(2, k) for k in every]
    slope = [m[k] * lam[k] for k in every]
    slope = [slope[k] + g[k] for k in every]
    inverse = [pl.reciprocal(slope[k], approx=True) for k in every]
    linear = [g[k] * lam[k] for k in every]
    cof = [coeffs(1, k) for k in every]
    linear = [linear[k] - cof[k] for k in every]
    quarter = [0.25 * m[k] for k in every]
    value = [quarter[k] * m[k] for k in every]
    value = [value[k] + linear[k] for k in every]
    beside()
    step = [value[k] * inverse[k] for k in every]
    return [lam[k] - step[k] for k in every]


def kernel(n, nr, total_rows, total_cols, row_hbm, col_hbm, st_hbm, basis_ref, image_ref,
           st_ref, rbuf, rraw, craw, cc, cn_ref, rn_ref, co_ref, acc, s_a, s_b, d_hi, d_lo, start, ssb, pout, part, agb, q_ref, lhs2,
           gx, uout, ub, ib,
           in_sem, ag_send, ag_recv, ss_send, ss_recv, pa_send, pa_recv, pg_send, pg_recv,
           gx_send, gx_recv, u_send, u_recv, i_send, i_recv):
    c, r = lax.axis_index("col"), lax.axis_index("row")
    line = n // 2
    z, x = c // 2, c % 2
    _, block_rows, atoms = row_hbm.shape
    cols = col_hbm.shape[1]
    vecs = st_hbm.shape[0]
    chunk = cols // nr
    tiles = cols // TILE

    def col_dev(k):
        return (r, k)

    def row_dev(k):
        return (k, c)

    def remote(src, dst, send, recv, dev):
        return pltpu.make_async_remote_copy(
            src_ref=src, dst_ref=dst, send_sem=send, recv_sem=recv, device_id=dev, device_id_type=MESH
        )

    loads = [
        pltpu.make_async_copy(row_hbm, rraw, in_sem.at[0]),
        pltpu.make_async_copy(col_hbm, craw, in_sem.at[1]),
        pltpu.make_async_copy(st_hbm, st_ref, in_sem.at[2]),
    ]
    for load in loads:
        load.start()

    barrier = pltpu.get_barrier_semaphore()
    for d in range(1, n):
        pl.semaphore_signal(barrier, inc=1, device_id=col_dev((c + d) % n), device_id_type=MESH)
    for d in range(1, nr):
        pl.semaphore_signal(barrier, inc=1, device_id=row_dev((r + d) % nr), device_id_type=MESH)
    loads[0].wait()
    for a in range(3):
        v = rraw[a].astype(F32)
        v = (v - jnp.sum(v, axis=1, keepdims=True) * (1.0 / atoms)).astype(BF16).astype(F32)
        rbuf[c, a] = (v * (1.0 / atoms)).astype(BF16)
    pl.semaphore_wait(barrier, n - 1 + nr - 1)

    half_rows = block_rows // 2

    def hop(block, half, way):
        dev = col_dev((c + 1 - 2 * x, c + 2, c - 2)[way])
        piece = rbuf.at[block, :, half * half_rows:(half + 1) * half_rows, :]
        return remote(piece, piece, ag_send.at[way, half, block], ag_recv.at[half, block], dev)

    def is_end(place):
        return (place == 0) | (place == line - 1)

    def line_hops(block, place, half, act):
        @pl.when((place <= z) & (z < line - 1))
        def _():
            act(hop(block, half, 1))

        @pl.when((place >= z) & (z > 0))
        def _():
            act(hop(block, half, 2))

    def hops(place, act):
        block = place * 2 + x
        for half in range(2):
            line_hops(block, place, half, act)
        act(hop(block, 0, 0))

        @pl.when(jnp.logical_not(is_end(place)) | (place == z))
        def _():
            act(hop(block, 1, 0))

    def crossed_hops(place, act):
        line_hops(place * 2 + 1 - x, place, 1, act)

    start_copy = lambda copy: copy.start()
    hops(z, start_copy)

    loads[2].wait()
    st = st_ref[...].T
    st_hi, st_lo = split(st)
    start[:, 0:vecs] = st_hi
    start[:, vecs:2 * vecs] = st_lo
    start[:, 2 * vecs:] = jnp.ones((cols, 128), BF16)
    ssb[c] = jnp.broadcast_to(jnp.sum(st, axis=0, keepdims=True), (8, vecs))

    def ss_copy(d):
        k = (c + d) % n
        return remote(ssb.at[c], ssb.at[c], ss_send.at[d], ss_recv.at[c], col_dev(k))

    for d in range(1, n):
        ss_copy(d).start()

    loads[1].wait()
    step_rows = 128

    def centre_cols(k, carry):
        at = pl.ds(pl.multiple_of(k * step_rows, step_rows), step_rows)
        squares = jnp.zeros((atoms, step_rows), F32)
        for b in range(3):
            v = craw[b, at, :].astype(F32)
            v = v - jnp.sum(v, axis=1, keepdims=True) * (1.0 / atoms)
            v = v.astype(BF16).T
            cc[b, :, at] = v
            v = v.astype(F32)
            squares = squares + v * v
        norm = jnp.sum(squares, axis=0, keepdims=True) * (0.5 / atoms)
        cn_ref[:, at] = jnp.broadcast_to(norm, (8, step_rows))
        return carry

    lax.fori_loop(0, cols // step_rows, centre_cols, 0)

    near = jnp.minimum(z, line - 1 - z)
    sign = jnp.where(z < line - 1 - z, 1, -1)

    def line_place(q):
        both = jnp.where(q % 2 == 1, (q + 1) // 2, -(q // 2))
        return z + jnp.where(q <= 2 * near, both, sign * (q - near))

    def part_copy(block):
        return remote(pout.at[block], part.at[c], pa_send.at[block], pa_recv.at[c], col_dev(block))

    def block_at(p):
        return line_place(p // 2) * 2 + jnp.where(p % 2 == 1, 1 - x, x)

    def norms(block, slot):
        squares = jnp.zeros((block_rows, atoms), F32)
        for a in range(3):
            v = rbuf[block, a].astype(F32)
            squares = squares + v * v
        norm = jnp.sum(squares, axis=1, keepdims=True) * (0.5 * atoms)
        rn_ref[slot] = jnp.broadcast_to(norm, (block_rows, 128))

    def cross(block, t, out, parts=range(3)):
        at = pl.ds(pl.multiple_of(t * TILE, TILE), TILE)
        rows = rbuf[block].reshape(3 * block_rows, atoms)
        for b in parts:
            out[b] = dot_nn(rows, cc[b, :, at])

    groups = [
        [(i, l) for i in range(i0, i0 + 32, 8) for l in range(0, TILE, 128)]
        for i0 in range(0, block_rows, 32)
    ]

    def solve_pair(block, slot, t, coming, first):
        def half(tile, i, l):
            cn = cn_ref[:, pl.ds(pl.multiple_of(tile * TILE + l, 128), 128)]
            return rn_ref[slot, i:i + 8, :] + cn

        def coeffs(turn, k, src, i, l):
            at = [slice(a * block_rows + i, a * block_rows + i + 8) for a in range(3)]
            terms = setup_terms([[src[b, at[a], l:l + 128] for b in range(3)] for a in range(3)])
            for kind in range(3):
                co_ref[turn, kind, k] = terms[kind]

        stream = [(t, s_a, g) for g in groups] + [(t + 1, s_b, g) for g in groups]
        for k, (i, l) in enumerate(groups[0]):
            coeffs(0, k, s_a, i, l)
        for index, (tile, _, group) in enumerate(stream):
            after = stream[index + 1] if index + 1 < len(stream) else None
            turn = index % 2
            place = index % len(groups)
            if index < len(groups):
                if place < min(3, len(groups) - 1):
                    cross(block, t + 1, s_b, range(place, 3, max(1, min(3, len(groups) - 1))))
                elif len(groups) == 1:
                    cross(block, t + 1, s_b)
            elif place < min(3, len(groups)):
                cross(coming, first, s_a, range(place, 3, min(3, len(groups))))
            lam = [half(tile, i, l) for i, l in group]
            for step in range(NEWTON):

                def beside():
                    if after is not None and step < len(after[2]):
                        coeffs(1 - turn, step, after[1], *after[2][step])

                lam = newton(lambda kind, k: co_ref[turn, kind, k], lam, beside)
            dist = {place: half(tile, *place) - v for place, v in zip(group, lam)}
            for i, l in group:
                if i % 16 == 0:
                    value = jnp.concatenate([dist[(i, l)], dist[(i + 8, l)]], axis=0)
                    at_rows = pl.ds(pl.multiple_of(block * block_rows + i, 16), 16)
                    at_cols = pl.ds(pl.multiple_of(tile * TILE + l, 128), 128)
                    high, low = split(value)
                    d_hi[at_rows, at_cols] = high
                    d_lo[at_rows, at_cols] = low

    span = 2 * TILE

    def panel_product(block, first, fresh):
        at = pl.ds(pl.multiple_of(block * block_rows, block_rows), block_rows)
        to = pl.ds(pl.multiple_of(first, span), span)
        value = dot_nn(d_hi[at, to], start[to, :]) + dot_nn(d_lo[at, to], start[to, :])
        acc[...] = jnp.where(fresh, value, acc[...] + value)

    def hand_over(block):
        both = acc[...].T
        pout[block, 0:vecs] = both[0:vecs] + both[vecs:2 * vecs]
        pout[block, vecs:vecs + 8] = both[2 * vecs:2 * vecs + 8]

        @pl.when(block == c)
        def _():
            part[c] = pout[block]

        @pl.when(block != c)
        def _():
            part_copy(block).start()

    def run_block(p, carry):
        block = block_at(p)
        coming = block_at(jnp.minimum(p + 1, n - 1))
        slot = p % 2

        def fetch():
            far = p // 2 + 1

            @pl.when((p % 2 == 0) & (far < line))
            def _():
                for place in (z + far, z - far):
                    @pl.when((place >= 0) & (place < line))
                    def _():
                        hop(place * 2 + x, 0, 0).wait_recv()
                        hop(place * 2 + x, 1, 0).wait_recv()
                        hops(place, start_copy)

            @pl.when(p % 2 == 0)
            def _():
                place = line_place(p // 2)
                hop(coming, 0, 0).wait_recv()

                @pl.when(jnp.logical_not(is_end(place)) | (place == z))
                def _():
                    hop(coming, 1, 0).wait_recv()

                @pl.when(is_end(place) & (place == z))
                def _():
                    crossed_hops(place, start_copy)

            @pl.when((p % 2 == 1) & (far < line))
            def _():
                for place, end in ((z + far, line - 1), (z - far, 0)):
                    @pl.when(place == end)
                    def _():
                        hop(place * 2 + 1 - x, 1, 0).wait_recv()
                        crossed_hops(place, start_copy)

        def pair(k, inner):
            t = 2 * k
            last = k == tiles // 2 - 1

            @pl.when(last & (p < n - 1))
            def _():
                fetch()
                norms(coming, 1 - slot)

            before = block_at(jnp.maximum(p - 1, 0))
            opening = k == 0
            panel_product(jnp.where(opening, before, block), jnp.where(opening, cols - span, (k - 1) * span), (k == 1) | (tiles == 2))
            solve_pair(block, slot, t, jnp.where(last, coming, block), jnp.where(last, 0, t + 2))

            @pl.when(opening & (p > 0))
            def _():
                hand_over(before)

            return inner

        lax.fori_loop(0, tiles // 2, pair, 0)

        return carry

    norms(c, 0)
    cross(c, 0, s_a)
    lax.fori_loop(0, n, run_block, 0)
    panel_product(block_at(n - 1), cols - span, tiles == 2)
    hand_over(block_at(n - 1))

    for d in range(1, n):
        k = (c + d) % n
        remote(ssb.at[k], ssb.at[k], ss_send.at[d], ss_recv.at[k], col_dev(k)).wait_recv()
        remote(pout.at[k], part.at[k], pa_send.at[k], pa_recv.at[k], col_dev(k)).wait_recv()
    summed, starts = part[0], ssb[0]
    for k in range(1, n):
        summed, starts = summed + part[k], starts + ssb[k]
    eye = lax.broadcasted_iota(jnp.int32, (vecs, vecs), 0) == lax.broadcasted_iota(jnp.int32, (vecs, vecs), 1)
    mean = jnp.sum(jnp.where(eye, jnp.broadcast_to(starts[0:1, :], (vecs, vecs)), 0.0), axis=1, keepdims=True)
    mean = mean * (1.0 / total_cols)
    agb[c, 0:vecs] = summed[0:vecs] - mean * summed[vecs:vecs + 1]
    agb[c, vecs:vecs + 8] = summed[vecs:vecs + 8]

    def pg_copy(d):
        return remote(agb.at[c], agb.at[c], pg_send.at[d], pg_recv.at[c], col_dev((c + d) % n))

    for d in range(1, n):
        pg_copy(d).start()
    for d in range(1, n):
        k = (c + d) % n
        remote(agb.at[k], agb.at[k], pg_send.at[d], pg_recv.at[k], col_dev(k)).wait_recv()

    local = n * block_rows
    for k in range(n):
        q_ref[:, k * block_rows:(k + 1) * block_rows] = agb[k]
    prod = q_ref[0:vecs, :]
    row_total = q_ref[vecs:vecs + 1, :]
    local_mean = jnp.sum(prod, axis=1, keepdims=True) * (1.0 / local)
    q = prod - local_mean
    q_ref[0:vecs, :] = q
    q_hi, q_lo = split(q)
    lhs2[0:vecs, :] = q_hi
    lhs2[vecs:2 * vecs, :] = q_lo
    lhs2[2 * vecs:2 * vecs + 16, :] = jnp.ones((16, local), BF16)
    gx[r, :, 0:vecs] = dot_nt(q, q, HIGHEST)
    lane = lax.broadcasted_iota(jnp.int32, (vecs, 128), 1)
    extra = jnp.where(lane == 0, local_mean, 0.0)
    extra = extra + jnp.where(lane == 1, jnp.sum(q * row_total, axis=1, keepdims=True), 0.0)
    extra = extra + jnp.where(lane == 2, jnp.sum(row_total, axis=1, keepdims=True), 0.0)
    gx[r, :, 128:256] = extra

    def gx_copy(d):
        return remote(gx.at[r], gx.at[r], gx_send.at[d], gx_recv.at[r], row_dev((r + d) % nr))

    for d in range(1, nr):
        gx_copy(d).start()

    def u_copy(d):
        o = (r + d) % nr
        return remote(uout.at[d], ub.at[r], u_send.at[d], u_recv.at[r], row_dev(o))

    for d in list(range(1, nr)) + [0]:
        o = (r + d) % nr
        at = pl.ds(pl.multiple_of(o * chunk, chunk), chunk)
        high = dot_nn(lhs2[...], d_hi[:, at])
        both = high + dot_nn(lhs2[...], d_lo[:, at])
        product = both[0:vecs] + both[vecs:2 * vecs]
        sums = both[2 * vecs:2 * vecs + 8]
        if d:
            uout[d, 0:vecs] = product
            uout[d, vecs:vecs + 8] = sums
            u_copy(d).start()
        else:
            ub[r, 0:vecs] = product
            ub[r, vecs:vecs + 8] = sums

    for d in range(1, nr):
        k = (r + d) % nr
        remote(gx.at[k], gx.at[k], gx_send.at[d], gx_recv.at[k], row_dev(k)).wait_recv()
    means = [gx[k, :, 128:129] for k in range(nr)]
    mean = sum(means) * (1.0 / nr)
    shift = jnp.zeros((vecs, 128), F32)
    gram = jnp.zeros((vecs, vecs), F32)
    weighted = jnp.zeros((vecs, 1), F32)
    for k in range(nr):
        gram = gram + gx[k, :, 0:vecs]
        shift = shift + jnp.where(lane == k, means[k] - mean, 0.0)
        weighted = weighted + gx[k, :, 129:130] + (means[k] - mean) * gx[k, :, 130:131]
    gram = (gram + float(local) * dot_nt(shift, shift, HIGHEST)) * (1.0 / total_rows)

    work = jnp.concatenate([gram, jnp.where(eye, 1.0, 0.0)], axis=1)
    below = lax.broadcasted_iota(jnp.int32, (vecs, 1), 0)
    ratio, scale = jnp.zeros((vecs, 1), F32), jnp.zeros((vecs, 1), F32)
    for k in range(0, vecs, 2):
        top, low = work[k:k + 1, :], work[k + 1:k + 2, :]
        left, right = work[:, k:k + 1], work[:, k + 1:k + 2]
        first, off, second = top[:, k:k + 1], top[:, k + 1:k + 2], low[:, k + 1:k + 2]
        inv = 1.0 / (first * second - off * off)
        ratio = jnp.where(below == k + 1, off / first, ratio)
        scale = jnp.where(below == k, first, jnp.where(below == k + 1, second - off * (off / first), scale))
        keep = jnp.where(below > k + 1, inv, 0.0)
        work = work - ((left * second - right * off) * keep) * top - ((right * first - left * off) * keep) * low
    unit = work[:, vecs:2 * vecs]
    above = jnp.concatenate([unit[vecs - 1:vecs, :], unit[0:vecs - 1, :]], axis=0)
    inverse = (unit - ratio * above) * lax.rsqrt(scale)

    own_mean = jnp.sum(jnp.where(lane == r, shift, 0.0), axis=1, keepdims=True)
    basis_ref[...] = -dot_nn(inverse, q_ref[0:vecs, :] + own_mean, HIGHEST)

    for d in range(1, nr):
        k = (r + d) % nr
        remote(uout.at[d], ub.at[k], u_send.at[d], u_recv.at[k], row_dev(k)).wait_recv()
    gathered = jnp.broadcast_to(weighted * (-1.0 / total_cols), (vecs, chunk))
    for k in range(nr):
        gathered = gathered + (ub[k, 0:vecs] + (means[k] - mean) * ub[k, vecs:vecs + 1])
    ib[r] = dot_nn(inverse, gathered, HIGHEST) * (1.0 / math.sqrt(total_rows))

    def i_copy(d):
        return remote(ib.at[r], ib.at[r], i_send.at[d], i_recv.at[r], row_dev((r + d) % nr))

    for d in range(1, nr):
        i_copy(d).start()
    for d in range(1, nr):
        k = (r + d) % nr
        remote(ib.at[k], ib.at[k], i_send.at[d], i_recv.at[k], row_dev(k)).wait_recv()
    for k in range(nr):
        image_ref[:, k * chunk:(k + 1) * chunk] = ib[k]

    for place in range(line):
        hops(place, lambda copy: copy.wait_send())
    for place in (0, line - 1):
        crossed_hops(place, lambda copy: copy.wait_send())
    for d in range(1, n):
        ss_copy(d).wait_send()
        pg_copy(d).wait_send()
        part_copy((c + d) % n).wait_send()
    for d in range(1, nr):
        gx_copy(d).wait_send()
        u_copy(d).wait_send()
        i_copy(d).wait_send()


def solution(mesh):
    n, nr = mesh.shape["col"], mesh.shape["row"]

    def body(row_coords, col_coords, start_block):
        _, block_rows, atoms = row_coords.shape
        cols, vecs = start_block.shape
        local = n * block_rows
        chunk = cols // nr
        dma = pltpu.SemaphoreType.DMA
        basis, image = pl.pallas_call(
            functools.partial(kernel, n, nr, local * nr, cols * n),
            out_shape=(
                jax.ShapeDtypeStruct((vecs, local), F32),
                jax.ShapeDtypeStruct((vecs, cols), F32),
            ),
            in_specs=[pl.BlockSpec(memory_space=pltpu.HBM)] * 3,
            out_specs=[pl.BlockSpec(memory_space=pltpu.VMEM)] * 2,
            scratch_shapes=[
                pltpu.VMEM((vecs, cols), F32),
                pltpu.VMEM((n, 3, block_rows, atoms), BF16),
                pltpu.VMEM((3, block_rows, atoms), BF16),
                pltpu.VMEM((3, cols, atoms), BF16),
                pltpu.VMEM((3, atoms, cols), BF16),
                pltpu.VMEM((8, cols), F32),
                pltpu.VMEM((2, block_rows, 128), F32),
                pltpu.VMEM((2, 3, 8, 8, 128), F32),
                pltpu.VMEM((block_rows, 2 * vecs + 128), F32),
                pltpu.VMEM((3, 3 * block_rows, TILE), F32),
                pltpu.VMEM((3, 3 * block_rows, TILE), F32),
                pltpu.VMEM((local, cols), BF16),
                pltpu.VMEM((local, cols), BF16),
                pltpu.VMEM((cols, 2 * vecs + 128), BF16),
                pltpu.VMEM((n, 8, vecs), F32),
                pltpu.VMEM((n, vecs + 8, block_rows), F32),
                pltpu.VMEM((n, vecs + 8, block_rows), F32),
                pltpu.VMEM((n, vecs + 8, block_rows), F32),
                pltpu.VMEM((vecs + 8, local), F32),
                pltpu.VMEM((2 * vecs + 16, local), BF16),
                pltpu.VMEM((nr, vecs, 256), F32),
                pltpu.VMEM((nr, vecs + 8, chunk), F32),
                pltpu.VMEM((nr, vecs + 8, chunk), F32),
                pltpu.VMEM((nr, vecs, chunk), F32),
                dma((3,)), dma((3, 2, n)), dma((2, n)), dma((n,)), dma((n,)), dma((n,)), dma((n,)), dma((n,)), dma((n,)),
                dma((nr,)), dma((nr,)), dma((nr,)), dma((nr,)), dma((nr,)), dma((nr,)),
            ],
            compiler_params=pltpu.CompilerParams(
                collective_id=0, has_side_effects=True, vmem_limit_bytes=54500 * 1024
            ),
        )(row_coords, col_coords, start_block.T)
        return (basis.T, image.T)

    in_specs = (P(None, ("row", "col"), None), P(None, "col", None), P("col", None))
    out_specs = (P("row", None), P("col", None))
    return jax.shard_map(body, mesh=mesh, in_specs=in_specs, out_specs=out_specs, check_vma=False)
```
